32 devices in a mesh: blk: 8 (over y, x, core), smp: 4 (over z).
Axes of the slice: x: 2, y: 2, z: 4, core: 2. Of those that a mesh axis runs over, the one named last changes fastest.
Arguments:
- field_tiles: bfloat16 [64, 262144], P(None, ('blk', 'smp')), may hold values from -6 to 6
- tile_dest: int32 [2048], replicated, may hold values from 0 to 2047, as said below
- near_cols: int32 [2048, 4], P(('blk', 'smp')), may hold values from 0 to 2047, as said below
- near_tiles: bfloat16 [2048, 4, 128, 128], P(('blk', 'smp')), may hold values from -0.25 to 0.25
- far_left: bfloat16 [5, 64, 262144], P(None, None, ('blk', 'smp')), may hold values from -0.3125 to 0.3125
- far_right: bfloat16 [5, 64, 262144], P(None, None, ('blk', 'smp')), may hold values from -6 to 6
Outputs:
- product: bfloat16 [64, 262144], P(None, ('blk', 'smp'))
The draws below stay inside these ranges and needn't reach their ends.
Inputs may be any that keep to these rules, and one draw needn't show every extreme that they name: tile_dest is a permutation of the blocks; the tiles of group g go to groups with the same value of g mod 4, exactly 8 of them to each such group. near_cols[b, 0] = b; every other entry lies within 8 of b.
All inputs are finite; a program needn't handle non-finite values.
Results may differ from the reference program's by a relative error of at most 0.0042.
Values may be sent and summed in bfloat16 or wider, within the bound.
A program may use at most 128 MiB of HBM per device.

```python
import jax
import jax.numpy as jnp
from jax import lax

BLOCK = 128
BPD = 64
SAMPLES = 64
RANK = 64
NEAR = 4
REACH = 8
LEVELS = 5
PTS_DEV = 8192
BLOCKS = 2048
POINTS = 262144
N_BLK = 8
N_SMP = 4
DEVICES = 32


def dest_group(key, smp_index):
    keys = jax.random.split(key, 4)
    perm_a = jax.random.permutation(keys[0], N_BLK)
    perm_b = jax.random.permutation(keys[1], N_BLK)
    perm_c = jax.random.permutation(keys[2], BPD)
    source_ids = jnp.arange(N_BLK, dtype=jnp.int32)[:, None]
    residue = (perm_b[source_ids] + perm_c[None, :]) % N_BLK
    dest_blk = perm_a[residue]
    arrival = source_ids * (BPD // N_BLK) + perm_c[None, :] // N_BLK
    slot_table = jax.vmap(lambda idx: jax.random.permutation(jax.random.fold_in(keys[3], idx), BPD))(jnp.arange(N_BLK, dtype=jnp.int32))
    slot_here = slot_table[dest_blk, arrival]
    return (dest_blk * N_SMP + smp_index) * BPD + slot_here


def draw_tile_dest(key, part):
    key = jax.random.fold_in(key, 11)
    groups = [dest_group(jax.random.fold_in(key, s_idx), s_idx) for s_idx in range(N_SMP)]
    return jnp.stack(groups, axis=1).reshape(BLOCKS).astype(jnp.int32)


def draw_near_cols(key, part):
    key = jax.random.fold_in(key, 7)
    row_ids = jnp.arange(BLOCKS, dtype=jnp.int32)[:, None]
    offsets = jax.random.randint(key, (BLOCKS, NEAR), -REACH, REACH + 1)
    offsets = offsets.at[:, 0].set(0)
    return jnp.clip(row_ids + offsets, 0, BLOCKS - 1).astype(jnp.int32)


def block_levels(key, shape, cuts, smallest, top_value):
    def one(axis_at, parts):
        draws = jax.random.uniform(jax.random.fold_in(jax.random.fold_in(key, 6), axis_at), (parts,), jnp.float32, smallest / len(cuts), top_value / len(cuts))
        return jnp.repeat(jnp.exp(draws), shape[axis_at] // parts).reshape((-1,) + (1,) * (len(shape) - axis_at - 1))

    factor_of = one(*cuts[0])
    for cut in cuts[1:]:
        factor_of = factor_of * one(*cut)
    return factor_of


def scatter_about(own_key, extent, scale, most, cuts=(), kind=jnp.bfloat16):
    factor_of = block_levels(own_key, extent, cuts, -0.22, 0.18) if cuts else 1.0
    result = jax.random.normal(own_key, extent, jnp.float32) * scale * factor_of
    return jnp.minimum(jnp.maximum(result, -most), most).astype(kind)


def setup_inputs(seed: int = 0) -> dict:
    key_of = jax.random.split(jax.random.key(seed), 7)
    return {
        "field_tiles": scatter_about(key_of[0], (SAMPLES, POINTS), 1.0, 6.0, ((1, 32),)),
        "tile_dest": draw_tile_dest(jax.random.fold_in(key_of[6], 71), 0),
        "near_cols": draw_near_cols(jax.random.fold_in(key_of[6], 71), 0),
        "near_tiles": scatter_about(key_of[3], (BLOCKS, NEAR, BLOCK, BLOCK), (NEAR * BLOCK) ** -0.5, 0.25, ((0, 32),)),
        "far_left": scatter_about(key_of[4], (LEVELS, RANK, POINTS), (RANK * LEVELS) ** -0.5, 0.3125, ((2, 32),)),
        "far_right": scatter_about(key_of[5], (LEVELS, RANK, POINTS), 1.0, 6.0, ((2, 32),)),
    }


def reference(field_tiles, tile_dest, near_cols, near_tiles, far_left, far_right):
    tile_rows = field_tiles.reshape(SAMPLES, BLOCKS, BLOCK)
    hilbert = jnp.zeros_like(tile_rows).at[:, tile_dest].set(tile_rows)
    cols_grouped = near_cols.reshape(DEVICES, BPD * NEAR)
    tiles_grouped = near_tiles.reshape(DEVICES, BPD, NEAR, BLOCK, BLOCK)

    def near_group(args):
        cols_here, tiles_here = args
        picked = jnp.take(hilbert, cols_here, axis=1).reshape(SAMPLES, BPD, NEAR, BLOCK)
        return jnp.einsum("sbkq,bkpq->sbp", picked.astype(jnp.float32), tiles_here.astype(jnp.float32))

    near_part = lax.map(near_group, (cols_grouped, tiles_grouped))
    near_part = near_part.transpose(1, 0, 2, 3).reshape(SAMPLES, POINTS)
    hil_dev = hilbert.reshape(SAMPLES, DEVICES, PTS_DEV).transpose(1, 0, 2)
    right_dev = far_right.reshape(LEVELS, RANK, DEVICES, PTS_DEV).transpose(2, 0, 1, 3)
    left_dev = far_left.reshape(LEVELS, RANK, DEVICES, PTS_DEV).transpose(2, 0, 1, 3)

    def project(args):
        right_here, hil_here = args
        return jnp.einsum("lrp,sp->lrs", right_here.astype(jnp.float32), hil_here.astype(jnp.float32))

    projection = lax.map(project, (right_dev, hil_dev))
    group_ids = jnp.arange(DEVICES, dtype=jnp.int32)
    couplings = []
    for level in range(LEVELS):
        span = DEVICES >> (level + 1)
        summed = projection[:, level].reshape(DEVICES // span, span, RANK, SAMPLES).sum(axis=1)
        partner = jnp.bitwise_xor(group_ids // span, 1)
        couplings.append(jnp.take(summed, partner, axis=0) * (float(span) * PTS_DEV) ** -0.5)
    coupling = jnp.stack(couplings, axis=1).astype(jnp.bfloat16)

    def expand(args):
        left_here, coupling_here = args
        return jnp.einsum("lrp,lrs->sp", left_here.astype(jnp.float32), coupling_here.astype(jnp.float32))

    far_part = lax.map(expand, (left_dev, coupling))
    far_part = far_part.transpose(1, 0, 2).reshape(SAMPLES, POINTS)
    return (near_part + far_part).astype(jnp.bfloat16)
```

```python
import functools

import jax
import jax.numpy as jnp
from jax import lax
from jax.experimental import pallas as pl
from jax.experimental.pallas import tpu as pltpu
from jax.sharding import PartitionSpec as P

BLOCK = 128
BPD = 64
RANK = 64
NEAR = 4
REACH = 8
LEVELS = 5
PARTS = 2
MESH = pl.DeviceIdType.MESH
F32 = jnp.float32
BF16 = jnp.bfloat16
NT = (((1,), (1,)), ((), ()))
NN = (((1,), (0,)), ((), ()))


def flipped(value, mask):
    bit = 1
    while bit <= mask:
        if mask & bit:
            value = value + bit - 2 * bit * ((value // bit) % 2)
        bit *= 2
    return value


def halves_swapped(x):
    return pltpu.roll(x, 64, 1)


def kernel(
    n_blk, n_smp, samples,
    field_h, dest_h, cols_h, near_h, left_h, right_h, out_h,
    field_v, tiles_v, near_v, left_v, right_v, dest_v, source_v, order_v, place_v,
    order_s, place_s, cols_s, acc, out_v, proj,
    *rest,
):
    per = samples // PARTS
    half = per // 2
    peer = BPD // n_blk
    blk_bits = n_blk.bit_length() - 1
    smp_levels = LEVELS - blk_bits
    points = BPD * BLOCK
    rest = list(rest)

    def take(n):
        got = rest[:n]
        del rest[:n]
        return got

    outgoing, arrived, hil, low, high = (take(PARTS) for _ in range(5))
    z_send, z_recv, b_send, b_recv = (take(PARTS) for _ in range(4))
    load_sem, a2a_send, a2a_recv, halo_send, halo_recv = take(5)
    zs_sem, zr_sem, bs_sem, br_sem, out_sem = take(5)

    blk = lax.axis_index("blk")
    smp = lax.axis_index("smp")
    me = blk * n_smp + smp

    def load(src, dst, at):
        copy = pltpu.make_async_copy(src, dst, load_sem.at[at])
        copy.start()
        return copy

    dest_load = load(dest_h, dest_v, 0)
    field_load = load(field_h, field_v, 1)
    cols_load = load(cols_h, cols_s, 2)

    following = ((blk + (smp + 1) // n_smp) % n_blk, (smp + 1) % n_smp)
    previous = (
        (blk + n_blk - 1 + (smp + n_smp - 1) // n_smp) % n_blk,
        (smp + n_smp - 1) % n_smp,
    )
    blk_peers = [(flipped(blk, j), smp) for j in range(1, n_blk)]
    smp_peers = [(blk, flipped(smp, j)) for j in range(1, n_smp)]
    everyone = blk_peers + smp_peers + [following, previous]
    barrier = pltpu.get_barrier_semaphore()
    for device in everyone:
        pl.semaphore_signal(barrier, inc=1, device_id=device, device_id_type=MESH)

    right_load = load(right_h, right_v, 3)
    near_load = load(near_h, near_v, 4)
    left_load = load(left_h, left_v, 5)

    rows = lax.broadcasted_iota(jnp.int32, (BPD, 128), 0)
    lanes = lax.broadcasted_iota(jnp.int32, (BPD, 128), 1)
    dest_load.wait()
    own = jnp.broadcast_to(dest_v[pl.ds(me, 1), :], (BPD, 128))
    target = lax.shift_right_arithmetic(own, (BPD * n_smp).bit_length() - 1)
    column = jnp.sum(jnp.where(rows == lanes, target, 0), axis=1, keepdims=True)
    before = jnp.where((target == column) & (lanes < rows), 1, 0)
    place = column * peer + jnp.sum(before, axis=1, keepdims=True)
    order = jnp.sum(jnp.where(place == lanes, rows, 0), axis=0, keepdims=True)
    order_v[...] = jnp.broadcast_to(order, (8, 128))
    order_copy = pltpu.make_async_copy(order_v, order_s, load_sem.at[6])
    order_copy.start()
    field_load.wait()

    def split(t, carry):
        at = pl.multiple_of(t * BLOCK, BLOCK)
        tiles_v[t] = field_v[:, pl.ds(at, BLOCK)]
        return carry

    lax.fori_loop(0, BPD, split, 0, unroll=8)
    order_copy.wait()

    def fill(part, j):
        group = flipped(blk, j)
        into = arrived[part] if j == 0 else outgoing[part]

        def body(i, carry):
            at = group * peer + i
            into[at] = tiles_v[order_s[0, at], pl.ds(part * per, per), :]
            return carry

        lax.fori_loop(0, peer, body, 0, unroll=True)

    def a2a(part, j):
        theirs = flipped(blk, j)
        return pltpu.make_async_remote_copy(
            src_ref=outgoing[part].at[pl.ds(theirs * peer, peer)],
            dst_ref=arrived[part].at[pl.ds(blk * peer, peer)],
            send_sem=a2a_send.at[part, j],
            recv_sem=a2a_recv.at[part, j],
            device_id=(theirs, smp),
            device_id_type=MESH,
        )

    sends = list(range(n_blk - 1, 0, -1))
    for at, j in enumerate(sends):
        fill(0, j)
        if at == 0:
            pl.semaphore_wait(barrier, len(everyone))
        a2a(0, j).start()
    for part in range(PARTS):
        fill(part, 0)
    for part in range(1, PARTS):
        for j in sends:
            fill(part, j)

    for s in range(n_blk):
        source_v[pl.ds(s, 1), :] = dest_v[pl.ds(s * n_smp + smp, 1), :]
    here = source_v[...] - me * BPD
    s_rows = lax.broadcasted_iota(jnp.int32, (n_blk, 128), 0)
    s_lanes = lax.broadcasted_iota(jnp.int32, (n_blk, 128), 1)
    mine = jnp.where((here >= 0) & (here < BPD), 1, 0)
    total = mine
    shift = 1
    while shift < BPD:
        total = total + jnp.where(s_lanes >= shift, pltpu.roll(total, shift, 1), 0)
        shift *= 2
    lands = s_rows * peer + total - mine
    found = jnp.zeros((BPD, 128), jnp.int32)
    for s in range(n_blk):
        found = found + jnp.where(here[s : s + 1, :] == rows, lands[s : s + 1, :], 0)
    found = jnp.sum(found, axis=1, keepdims=True)
    found = jnp.sum(jnp.where(rows == lanes, found, 0), axis=0, keepdims=True)
    found = jnp.minimum(jnp.maximum(found, 0), BPD - 1)
    place_v[...] = jnp.broadcast_to(found, (8, 128))
    place_copy = pltpu.make_async_copy(place_v, place_s, load_sem.at[7])
    place_copy.start()
    place_copy.wait()
    cols_load.wait()

    lane = lax.broadcasted_iota(jnp.int32, (per, 128), 1) < 64
    lane_half = lax.broadcasted_iota(jnp.int32, (half, 128), 1) < 64

    def halo(part, up):
        source = hil[part].at[pl.ds(BPD - REACH, REACH) if up else pl.ds(0, REACH)]
        target_ref = low[part].at[pl.ds(0, REACH)] if up else high[part].at[pl.ds(2 * REACH, REACH)]
        return pltpu.make_async_remote_copy(
            src_ref=source,
            dst_ref=target_ref,
            send_sem=halo_send.at[part, int(up)],
            recv_sem=halo_recv.at[part, int(up)],
            device_id=following if up else previous,
            device_id_type=MESH,
        )

    def z_kind(j):
        return 1 if smp_levels and j == 1 else 0

    def z_copy(part, j):
        return pltpu.make_async_remote_copy(
            src_ref=z_send[part].at[z_kind(j)],
            dst_ref=z_recv[part].at[j],
            send_sem=zs_sem.at[part, j],
            recv_sem=zr_sem.at[part, j],
            device_id=(blk, flipped(smp, j)),
            device_id_type=MESH,
        )

    def b_level(j):
        return blk_bits - j.bit_length()

    def b_copy(part, j):
        return pltpu.make_async_remote_copy(
            src_ref=b_send[part].at[b_level(j)],
            dst_ref=b_recv[part].at[j],
            send_sem=bs_sem.at[part, j],
            recv_sem=br_sem.at[part, j],
            device_id=(flipped(blk, j), smp),
            device_id_type=MESH,
        )

    def gather(part):
        for j in sends:
            a2a(part, j).wait_recv()

        def edge(b, carry):
            first = arrived[part][place_s[0, b]]
            hil[part][b] = first
            low[part][b + REACH] = first
            final = arrived[part][place_s[0, b + BPD - 2 * REACH]]
            hil[part][b + BPD - 2 * REACH] = final
            high[part][b] = final
            return carry

        lax.fori_loop(0, 2 * REACH, edge, 0, unroll=4)
        halo(part, True).start()
        halo(part, False).start()

        def middle(b, carry):
            hil[part][b] = arrived[part][place_s[0, b]]
            return carry

        lax.fori_loop(2 * REACH, BPD - 2 * REACH, middle, 0, unroll=4)

    def project(part):
        proj[...] = jnp.zeros_like(proj)
        group = 8

        def step(i, carry):
            b = i * group
            block = jnp.concatenate([hil[part][b + k] for k in range(group)], axis=1)
            at = pl.multiple_of(i * group * BLOCK, group * BLOCK)
            proj[0 : LEVELS * RANK, 0:per] += lax.dot_general(
                right_v[:, pl.ds(at, group * BLOCK)], block, NT, preferred_element_type=F32
            )
            return carry

        lax.fori_loop(0, BPD // group, step, 0)
        sums = proj[...].T[0:per, :]
        tiles = [sums[:, k * 128 : (k + 1) * 128] for k in range(3)]
        if smp_levels:
            other = jnp.where(lane, tiles[1], halves_swapped(tiles[2]))
            z_send[part][0] = jnp.concatenate(tiles[:2], axis=1).astype(BF16)
            z_send[part][1] = jnp.concatenate([tiles[0], other], axis=1).astype(BF16)
        else:
            z_send[part][0] = sums.astype(BF16)
        for j in range(n_smp - 1, 0, -1):
            z_copy(part, j).start()
        return tiles

    def packed(x, level):
        top, bottom = x[0:half], x[half:per]
        if level % 2 == 0:
            return jnp.where(lane_half, top, halves_swapped(bottom))
        return jnp.where(lane_half, halves_swapped(top), bottom)

    def unpacked(x, level):
        if level % 2 == 0:
            return jnp.concatenate([x, halves_swapped(x)], axis=0)
        return jnp.concatenate([halves_swapped(x), x], axis=0)

    def reduce_smp(part, tiles):
        for j in range(1, n_smp):
            z_copy(part, j).wait_recv()
        got = {j: z_recv[part][j].astype(F32) for j in range(1, n_smp)}
        for level in range(blk_bits):
            t = level // 2
            if level % 2 == 0:
                summed = tiles[t]
                for j in range(1, n_smp):
                    summed = summed + got[j][:, t * 128 : (t + 1) * 128]
            b_send[part][level] = packed(summed, level).astype(BF16)
        for j in sends:
            b_copy(part, j).start()
        if not smp_levels:
            return None
        return got[1][:, 128:256], got[2][:, 128:256] + got[3][:, 128:256]

    def couple(part, inner):
        for j in sends:
            b_copy(part, j).wait_recv()
        by_level = []
        for level in range(blk_bits):
            total = None
            for j in range(1, n_blk):
                if b_level(j) == level:
                    one = b_recv[part][j].astype(F32)
                    total = one if total is None else total + one
            by_level.append(unpacked(total, level))
        if smp_levels:
            by_level.append(inner[1])
            by_level.append(halves_swapped(inner[0]))
        devices = n_blk * n_smp
        scales = [(float(devices >> level + 1) * points) ** -0.5 for level in range(LEVELS)]
        by_level = [x * s for x, s in zip(by_level, scales)]
        first = jnp.where(lane, by_level[0], by_level[1]).astype(BF16)
        second = jnp.where(lane, by_level[2], by_level[3]).astype(BF16)
        third = by_level[4].astype(BF16)[:, 0:RANK]
        return jnp.concatenate([first, second], axis=1), third

    def near_rows(part, source, start, stop):
        def body(b, carry):
            picks = []
            for k in range(NEAR):
                picks.append(source[cols_s[b * NEAR + k]])
            picked = jnp.concatenate(picks, axis=1)
            tile = jnp.concatenate([near_v[b, k] for k in range(NEAR)], axis=1)
            acc[pl.ds(part * per, per), pl.ds(pl.multiple_of(b * BLOCK, BLOCK), BLOCK)] = (
                lax.dot_general(picked, tile, NT, preferred_element_type=F32)
            )
            return carry

        lax.fori_loop(start, stop, body, 0, unroll=4)

    wide = 512
    pieces = 4

    def out_copy(part, piece):
        where = (pl.ds(part * per, per), pl.ds(piece * (points // pieces), points // pieces))
        return pltpu.make_async_copy(out_v.at[where], out_h.at[where], out_sem.at[part, piece])

    def far(part, coupling):
        first, last = coupling

        def body(i, carry):
            at = pl.ds(pl.multiple_of(i * wide, wide), wide)
            value = lax.dot_general(
                first, left_v[0 : 4 * RANK, at], NN, preferred_element_type=F32
            ) + lax.dot_general(
                last, left_v[4 * RANK : 5 * RANK, at], NN, preferred_element_type=F32
            )
            mine = pl.ds(part * per, per)
            out_v[mine, at] = (acc[mine, at] + value).astype(BF16)
            return carry

        for piece in range(pieces):
            steps = points // pieces // wide
            lax.fori_loop(piece * steps, (piece + 1) * steps, body, 0, unroll=2)
            out_copy(part, piece).start()

    for part in range(PARTS):
        gather(part)
        if part + 1 < PARTS:
            for j in sends:
                a2a(part, j).wait_send()
                a2a(part + 1, j).start()
        if part == 0:
            right_load.wait()
        tiles = project(part)
        if part == 0:
            near_load.wait()
        middle_row = BPD // 2
        near_rows(part, hil[part], REACH, middle_row)
        inner = reduce_smp(part, tiles)
        near_rows(part, hil[part], middle_row, BPD - REACH)
        halo(part, True).wait_recv()
        halo(part, False).wait_recv()
        near_rows(part, low[part], 0, REACH)
        near_rows(part, high[part], BPD - REACH, BPD)
        if part == 0:
            left_load.wait()
        far(part, couple(part, inner))

    for j in sends:
        a2a(PARTS - 1, j).wait_send()
    for part in range(PARTS):
        halo(part, True).wait_send()
        halo(part, False).wait_send()
        for j in range(1, n_smp):
            z_copy(part, j).wait_send()
        for j in sends:
            b_copy(part, j).wait_send()
        for piece in range(pieces):
            out_copy(part, piece).wait()


def shards(field_tiles, tile_dest, near_cols, near_tiles, far_left, far_right):
    samples, points = field_tiles.shape
    n_blk = lax.axis_size("blk")
    n_smp = lax.axis_size("smp")
    devices = n_blk * n_smp
    per = samples // PARTS
    blk_bits = n_blk.bit_length() - 1
    smp_levels = LEVELS - blk_bits
    z_wide = 256 if smp_levels else 384
    dest = jnp.pad(tile_dest.reshape(devices, BPD), ((0, 0), (0, 128 - BPD)), constant_values=-1)
    me = lax.axis_index("blk") * n_smp + lax.axis_index("smp")
    row = jnp.arange(BPD, dtype=jnp.int32)[:, None]
    base = jnp.where(row < REACH, -REACH, jnp.where(row < BPD - REACH, 0, BPD - 2 * REACH))
    most = jnp.where((row < REACH) | (row >= BPD - REACH), 3 * REACH, BPD) - 1
    cols = jnp.clip(near_cols - me * BPD - base, 0, most).reshape(-1)
    vmem = pltpu.VMEM
    dma = pltpu.SemaphoreType.DMA
    scratch = [
        vmem((samples, points), BF16),
        vmem((BPD, samples, BLOCK), BF16),
        vmem((BPD, NEAR, BLOCK, BLOCK), BF16),
        vmem((LEVELS * RANK, points), BF16),
        vmem((LEVELS * RANK, points), BF16),
        vmem((devices, 128), jnp.int32),
        vmem((n_blk, 128), jnp.int32),
        vmem((8, 128), jnp.int32),
        vmem((8, 128), jnp.int32),
        pltpu.SMEM((8, 128), jnp.int32),
        pltpu.SMEM((8, 128), jnp.int32),
        pltpu.SMEM((BPD * NEAR,), jnp.int32),
        vmem((samples, points), F32),
        vmem((samples, points), BF16),
        vmem((384, 128), F32),
    ]
    scratch += [vmem((BPD, per, BLOCK), BF16) for _ in range(3 * PARTS)]
    scratch += [vmem((3 * REACH, per, BLOCK), BF16) for _ in range(2 * PARTS)]
    scratch += [vmem((2, per, z_wide), BF16) for _ in range(PARTS)]
    scratch += [vmem((n_smp, per, z_wide), BF16) for _ in range(PARTS)]
    scratch += [vmem((blk_bits, per // 2, 128), BF16) for _ in range(PARTS)]
    scratch += [vmem((n_blk, per // 2, 128), BF16) for _ in range(PARTS)]
    scratch += [
        dma((8,)),
        dma((PARTS, n_blk)), dma((PARTS, n_blk)),
        dma((PARTS, 2)), dma((PARTS, 2)),
        dma((PARTS, n_smp)), dma((PARTS, n_smp)),
        dma((PARTS, n_blk)), dma((PARTS, n_blk)),
        dma((PARTS, 4)),
    ]
    anywhere = pl.BlockSpec(memory_space=pl.ANY)
    return pl.pallas_call(
        functools.partial(kernel, n_blk, n_smp, samples),
        out_shape=jax.ShapeDtypeStruct((samples, points), BF16),
        in_specs=[anywhere] * 6,
        out_specs=anywhere,
        scratch_shapes=scratch,
        compiler_params=pltpu.CompilerParams(
            collective_id=0, has_side_effects=True, vmem_limit_bytes=48 * 1024 * 1024
        ),
        cost_estimate=pl.CostEstimate(
            flops=1_300_000_000, bytes_accessed=22_000_000, transcendentals=0
        ),
    )(
        field_tiles,
        dest,
        cols,
        near_tiles,
        far_left.reshape(LEVELS * RANK, points),
        far_right.reshape(LEVELS * RANK, points),
    )


def solution(mesh):
    return jax.shard_map(
        shards,
        mesh=mesh,
        in_specs=(
            P(None, ("blk", "smp")),
            P(),
            P(("blk", "smp"), None),
            P(("blk", "smp"), None, None, None),
            P(None, None, ("blk", "smp")),
            P(None, None, ("blk", "smp")),
        ),
        out_specs=P(None, ("blk", "smp")),
        check_vma=False,
    )
```

```python
import functools

import jax
import jax.numpy as jnp
from jax import lax
from jax.experimental import pallas as pl
from jax.experimental.pallas import tpu as pltpu
from jax.sharding import PartitionSpec as P

BLOCK = 128
BPD = 64
RANK = 64
NEAR = 4
REACH = 8
LEVELS = 5
PARTS = 2
MESH = pl.DeviceIdType.MESH
F32 = jnp.float32
BF16 = jnp.bfloat16
NT = (((1,), (1,)), ((), ()))
NN = (((1,), (0,)), ((), ()))


def flipped(value, mask):
    bit = 1
    while bit <= mask:
        if mask & bit:
            value = value + bit - 2 * bit * ((value // bit) % 2)
        bit *= 2
    return value


def halves_swapped(x):
    return pltpu.roll(x, 64, 1)


def kernel(
    n_blk, n_smp, samples,
    field_h, dest_h, cols_h, near_h, left_h, right_h, out_h,
    field_v, tiles_v, near_v, left_v, right_v, dest_v, cols_v, source_v, order_v, place_v,
    order_s, place_s, acc, out_v, proj,
    *rest,
):
    per = samples // PARTS
    half = per // 2
    peer = BPD // n_blk
    blk_bits = n_blk.bit_length() - 1
    smp_levels = LEVELS - blk_bits
    points = BPD * BLOCK
    rest = list(rest)

    def take(n):
        got = rest[:n]
        del rest[:n]
        return got

    outgoing, arrived, hil, low, high = (take(PARTS) for _ in range(5))
    z_send, z_recv, b_send, b_recv = (take(PARTS) for _ in range(4))
    load_sem, a2a_send, a2a_recv, halo_send, halo_recv = take(5)
    zs_sem, zr_sem, bs_sem, br_sem, out_sem = take(5)

    blk = lax.axis_index("blk")
    smp = lax.axis_index("smp")
    me = blk * n_smp + smp

    def load(src, dst, at):
        copy = pltpu.make_async_copy(src, dst, load_sem.at[at])
        copy.start()
        return copy

    dest_load = load(dest_h, dest_v, 0)
    field_load = load(field_h, field_v, 1)
    cols_load = load(cols_h, cols_v, 2)

    following = ((blk + (smp + 1) // n_smp) % n_blk, (smp + 1) % n_smp)
    previous = (
        (blk + n_blk - 1 + (smp + n_smp - 1) // n_smp) % n_blk,
        (smp + n_smp - 1) % n_smp,
    )
    blk_peers = [(flipped(blk, j), smp) for j in range(1, n_blk)]
    smp_peers = [(blk, flipped(smp, j)) for j in range(1, n_smp)]
    everyone = blk_peers + smp_peers + [following, previous]
    barrier = pltpu.get_barrier_semaphore()
    for device in everyone:
        pl.semaphore_signal(barrier, inc=1, device_id=device, device_id_type=MESH)

    right_load = load(right_h, right_v, 3)
    near_load = load(near_h, near_v, 4)
    left_load = load(left_h, left_v, 5)

    rows = lax.broadcasted_iota(jnp.int32, (BPD, 128), 0)
    lanes = lax.broadcasted_iota(jnp.int32, (BPD, 128), 1)
    dest_load.wait()
    own = jnp.broadcast_to(dest_v[pl.ds(me // 2, 1), :], (BPD, 128))
    own = jnp.where(lanes < BPD, pltpu.roll(own, 64 * (me % 2), 1), -1)
    target = lax.shift_right_arithmetic(own, (BPD * n_smp).bit_length() - 1)
    column = jnp.sum(jnp.where(rows == lanes, target, 0), axis=1, keepdims=True)
    before = jnp.where((target == column) & (lanes < rows), 1, 0)
    place = column * peer + jnp.sum(before, axis=1, keepdims=True)
    order = jnp.sum(jnp.where(place == lanes, rows, 0), axis=0, keepdims=True)
    order_v[...] = jnp.broadcast_to(order, (8, 128))
    order_copy = pltpu.make_async_copy(order_v, order_s, load_sem.at[6])
    order_copy.start()
    field_load.wait()

    def split(t, carry):
        at = pl.multiple_of(t * BLOCK, BLOCK)
        tiles_v[t] = field_v[:, pl.ds(at, BLOCK)]
        return carry

    lax.fori_loop(0, BPD, split, 0, unroll=8)
    order_copy.wait()

    def fill(part, j):
        group = flipped(blk, j)
        into = arrived[part] if j == 0 else outgoing[part]

        def body(i, carry):
            at = group * peer + i
            into[at] = tiles_v[order_s[0, at], pl.ds(part * per, per), :]
            return carry

        lax.fori_loop(0, peer, body, 0, unroll=True)

    def a2a(part, j):
        theirs = flipped(blk, j)
        return pltpu.make_async_remote_copy(
            src_ref=outgoing[part].at[pl.ds(theirs * peer, peer)],
            dst_ref=arrived[part].at[pl.ds(blk * peer, peer)],
            send_sem=a2a_send.at[part, j],
            recv_sem=a2a_recv.at[part, j],
            device_id=(theirs, smp),
            device_id_type=MESH,
        )

    sends = list(range(n_blk - 1, 0, -1))
    for at, j in enumerate(sends):
        fill(0, j)
        if at == 0:
            pl.semaphore_wait(barrier, len(everyone))
        a2a(0, j).start()
    for part in range(PARTS):
        fill(part, 0)
    for part in range(1, PARTS):
        for j in sends:
            fill(part, j)

    for s in range(n_blk):
        source_v[pl.ds(s, 1), :] = dest_v[pl.ds((s * n_smp + smp) // 2, 1), :]
    here = pltpu.roll(source_v[...], 64 * (smp % 2), 1) - me * BPD
    s_rows = lax.broadcasted_iota(jnp.int32, (n_blk, 128), 0)
    s_lanes = lax.broadcasted_iota(jnp.int32, (n_blk, 128), 1)
    here = jnp.where(s_lanes < BPD, here, -1)
    mine = jnp.where((here >= 0) & (here < BPD), 1, 0)
    total = mine
    shift = 1
    while shift < BPD:
        total = total + jnp.where(s_lanes >= shift, pltpu.roll(total, shift, 1), 0)
        shift *= 2
    lands = s_rows * peer + total - mine
    found = jnp.zeros((BPD, 128), jnp.int32)
    for s in range(n_blk):
        found = found + jnp.where(here[s : s + 1, :] == rows, lands[s : s + 1, :], 0)
    found = jnp.sum(found, axis=1, keepdims=True)
    found = jnp.sum(jnp.where(rows == lanes, found, 0), axis=0, keepdims=True)
    found = jnp.minimum(jnp.maximum(found, 0), BPD - 1)
    place_v[...] = jnp.broadcast_to(found, (8, 128))
    cols_load.wait()
    c_lanes = lax.broadcasted_iota(jnp.int32, (NEAR, BPD), 1)
    inner_row = (c_lanes >= REACH) & (c_lanes < BPD - REACH)
    base = jnp.where(inner_row, 0, jnp.where(c_lanes < REACH, -REACH, BPD - 2 * REACH))
    most = jnp.where(inner_row, BPD, 3 * REACH) - 1
    place_v[0:NEAR, 0:BPD] = jnp.minimum(jnp.maximum(cols_v[...] - me * BPD - base, 0), most)
    place_copy = pltpu.make_async_copy(place_v, place_s, load_sem.at[7])
    place_copy.start()
    place_copy.wait()

    lane = lax.broadcasted_iota(jnp.int32, (per, 128), 1) < 64
    lane_half = lax.broadcasted_iota(jnp.int32, (half, 128), 1) < 64

    def halo(part, up):
        source = hil[part].at[pl.ds(BPD - REACH, REACH) if up else pl.ds(0, REACH)]
        target_ref = low[part].at[pl.ds(0, REACH)] if up else high[part].at[pl.ds(2 * REACH, REACH)]
        return pltpu.make_async_remote_copy(
            src_ref=source,
            dst_ref=target_ref,
            send_sem=halo_send.at[part, int(up)],
            recv_sem=halo_recv.at[part, int(up)],
            device_id=following if up else previous,
            device_id_type=MESH,
        )

    def z_kind(j):
        return 1 if smp_levels and j == 1 else 0

    def z_copy(part, j):
        return pltpu.make_async_remote_copy(
            src_ref=z_send[part].at[z_kind(j)],
            dst_ref=z_recv[part].at[j],
            send_sem=zs_sem.at[part, j],
            recv_sem=zr_sem.at[part, j],
            device_id=(blk, flipped(smp, j)),
            device_id_type=MESH,
        )

    def b_level(j):
        return blk_bits - j.bit_length()

    def b_copy(part, j):
        return pltpu.make_async_remote_copy(
            src_ref=b_send[part].at[b_level(j)],
            dst_ref=b_recv[part].at[j],
            send_sem=bs_sem.at[part, j],
            recv_sem=br_sem.at[part, j],
            device_id=(flipped(blk, j), smp),
            device_id_type=MESH,
        )

    def gather(part):
        def edge(b, carry):
            first = arrived[part][place_s[NEAR, b]]
            hil[part][b] = first
            low[part][b + REACH] = first
            final = arrived[part][place_s[NEAR, b + BPD - 2 * REACH]]
            hil[part][b + BPD - 2 * REACH] = final
            high[part][b] = final
            return carry

        lax.fori_loop(0, 2 * REACH, edge, 0, unroll=4)
        halo(part, True).start()
        halo(part, False).start()

        def middle(b, carry):
            hil[part][b] = arrived[part][place_s[NEAR, b]]
            return carry

        lax.fori_loop(2 * REACH, BPD - 2 * REACH, middle, 0, unroll=4)

    def project(part):
        proj[...] = jnp.zeros_like(proj)
        group = 8

        def step(i, carry):
            b = i * group
            block = jnp.concatenate([hil[part][b + k] for k in range(group)], axis=1)
            at = pl.multiple_of(i * group * BLOCK, group * BLOCK)
            proj[0 : LEVELS * RANK, 0:per] += lax.dot_general(
                right_v[:, pl.ds(at, group * BLOCK)], block, NT, preferred_element_type=F32
            )
            return carry

        lax.fori_loop(0, BPD // group, step, 0)
        sums = proj[...].T[0:per, :]
        tiles = [sums[:, k * 128 : (k + 1) * 128] for k in range(3)]
        if smp_levels:
            other = jnp.where(lane, tiles[1], halves_swapped(tiles[2]))
            z_send[part][0] = jnp.concatenate(tiles[:2], axis=1).astype(BF16)
            z_send[part][1] = jnp.concatenate([tiles[0], other], axis=1).astype(BF16)
        else:
            z_send[part][0] = sums.astype(BF16)
        for j in range(n_smp - 1, 0, -1):
            z_copy(part, j).start()
        return tiles

    def packed(x, level):
        top, bottom = x[0:half], x[half:per]
        if level % 2 == 0:
            return jnp.where(lane_half, top, halves_swapped(bottom))
        return jnp.where(lane_half, halves_swapped(top), bottom)

    def unpacked(x, level):
        if level % 2 == 0:
            return jnp.concatenate([x, halves_swapped(x)], axis=0)
        return jnp.concatenate([halves_swapped(x), x], axis=0)

    def reduce_smp(part, tiles):
        for j in range(1, n_smp):
            z_copy(part, j).wait_recv()
        got = {j: z_recv[part][j].astype(F32) for j in range(1, n_smp)}
        for level in range(blk_bits):
            t = level // 2
            if level % 2 == 0:
                summed = tiles[t]
                for j in range(1, n_smp):
                    summed = summed + got[j][:, t * 128 : (t + 1) * 128]
            b_send[part][level] = packed(summed, level).astype(BF16)
        for j in sends:
            b_copy(part, j).start()
        if not smp_levels:
            return None
        return got[1][:, 128:256], got[2][:, 128:256] + got[3][:, 128:256]

    def couple(part, inner):
        for j in sends:
            b_copy(part, j).wait_recv()
        by_level = []
        for level in range(blk_bits):
            total = None
            for j in range(1, n_blk):
                if b_level(j) == level:
                    one = b_recv[part][j].astype(F32)
                    total = one if total is None else total + one
            by_level.append(unpacked(total, level))
        if smp_levels:
            by_level.append(inner[1])
            by_level.append(halves_swapped(inner[0]))
        devices = n_blk * n_smp
        scales = [(float(devices >> level + 1) * points) ** -0.5 for level in range(LEVELS)]
        by_level = [x * s for x, s in zip(by_level, scales)]
        first = jnp.where(lane, by_level[0], by_level[1]).astype(BF16)
        second = jnp.where(lane, by_level[2], by_level[3]).astype(BF16)
        third = by_level[4].astype(BF16)[:, 0:RANK]
        return jnp.concatenate([first, second], axis=1), third

    def near_rows(sources, start, stop):
        def body(b, carry):
            picks = []
            for k in range(NEAR):
                at = place_s[k, b]
                picks.append(jnp.concatenate([source[at] for source in sources], axis=0))
            picked = jnp.concatenate(picks, axis=1)
            tile = jnp.concatenate([near_v[b, k] for k in range(NEAR)], axis=1)
            acc[:, pl.ds(pl.multiple_of(b * BLOCK, BLOCK), BLOCK)] = lax.dot_general(
                picked, tile, NT, preferred_element_type=F32
            )
            return carry

        lax.fori_loop(start, stop, body, 0, unroll=4)

    wide = 512
    pieces = 4

    def out_copy(piece):
        where = (slice(None), pl.ds(piece * (points // pieces), points // pieces))
        return pltpu.make_async_copy(out_v.at[where], out_h.at[where], out_sem.at[piece])

    def far(couplings):
        first = jnp.concatenate([c[0] for c in couplings], axis=0)
        last = jnp.concatenate([c[1] for c in couplings], axis=0)

        def body(i, carry):
            at = pl.ds(pl.multiple_of(i * wide, wide), wide)
            value = lax.dot_general(
                first, left_v[0 : 4 * RANK, at], NN, preferred_element_type=F32
            ) + lax.dot_general(
                last, left_v[4 * RANK : 5 * RANK, at], NN, preferred_element_type=F32
            )
            out_v[:, at] = (acc[:, at] + value).astype(BF16)
            return carry

        for piece in range(pieces):
            steps = points // pieces // wide
            lax.fori_loop(piece * steps, (piece + 1) * steps, body, 0, unroll=2)
            out_copy(piece).start()

    tiles = [None] * PARTS
    inner = [None] * PARTS
    for part in range(PARTS):
        if part + 1 < PARTS:
            for j in sends:
                a2a(part, j).wait_send()
                a2a(part + 1, j).start()
        for j in sends:
            a2a(part, j).wait_recv()
        gather(part)
        if part == 0:
            right_load.wait()
        tiles[part] = project(part)
        if part > 0:
            inner[part - 1] = reduce_smp(part - 1, tiles[part - 1])
    near_load.wait()
    middle_row = BPD // 2
    near_rows(hil, REACH, middle_row)
    inner[PARTS - 1] = reduce_smp(PARTS - 1, tiles[PARTS - 1])
    near_rows(hil, middle_row, BPD - REACH)
    for part in range(PARTS):
        halo(part, True).wait_recv()
        halo(part, False).wait_recv()
    near_rows(low, 0, REACH)
    near_rows(high, BPD - REACH, BPD)
    left_load.wait()
    far([couple(part, inner[part]) for part in range(PARTS)])

    for j in sends:
        a2a(PARTS - 1, j).wait_send()
    for part in range(PARTS):
        halo(part, True).wait_send()
        halo(part, False).wait_send()
        for j in range(1, n_smp):
            z_copy(part, j).wait_send()
        for j in sends:
            b_copy(part, j).wait_send()
    for piece in range(pieces):
        out_copy(piece).wait()


def shards(field_tiles, tile_dest, near_cols, near_tiles, far_left, far_right):
    samples, points = field_tiles.shape
    n_blk = lax.axis_size("blk")
    n_smp = lax.axis_size("smp")
    devices = n_blk * n_smp
    per = samples // PARTS
    blk_bits = n_blk.bit_length() - 1
    smp_levels = LEVELS - blk_bits
    z_wide = 256 if smp_levels else 384
    vmem = pltpu.VMEM
    dma = pltpu.SemaphoreType.DMA
    scratch = [
        vmem((samples, points), BF16),
        vmem((BPD, samples, BLOCK), BF16),
        vmem((BPD, NEAR, BLOCK, BLOCK), BF16),
        vmem((LEVELS * RANK, points), BF16),
        vmem((LEVELS * RANK, points), BF16),
        vmem((devices * BPD // 128, 128), jnp.int32),
        vmem((NEAR, BPD), jnp.int32),
        vmem((n_blk, 128), jnp.int32),
        vmem((8, 128), jnp.int32),
        vmem((8, 128), jnp.int32),
        pltpu.SMEM((8, 128), jnp.int32),
        pltpu.SMEM((8, 128), jnp.int32),
        vmem((samples, points), F32),
        vmem((samples, points), BF16),
        vmem((384, 128), F32),
    ]
    scratch += [vmem((BPD, per, BLOCK), BF16) for _ in range(3 * PARTS)]
    scratch += [vmem((3 * REACH, per, BLOCK), BF16) for _ in range(2 * PARTS)]
    scratch += [vmem((2, per, z_wide), BF16) for _ in range(PARTS)]
    scratch += [vmem((n_smp, per, z_wide), BF16) for _ in range(PARTS)]
    scratch += [vmem((blk_bits, per // 2, 128), BF16) for _ in range(PARTS)]
    scratch += [vmem((n_blk, per // 2, 128), BF16) for _ in range(PARTS)]
    scratch += [
        dma((8,)),
        dma((PARTS, n_blk)), dma((PARTS, n_blk)),
        dma((PARTS, 2)), dma((PARTS, 2)),
        dma((PARTS, n_smp)), dma((PARTS, n_smp)),
        dma((PARTS, n_blk)), dma((PARTS, n_blk)),
        dma((4,)),
    ]
    anywhere = pl.BlockSpec(memory_space=pl.ANY)
    return pl.pallas_call(
        functools.partial(kernel, n_blk, n_smp, samples),
        out_shape=jax.ShapeDtypeStruct((samples, points), BF16),
        in_specs=[anywhere] * 6,
        out_specs=anywhere,
        scratch_shapes=scratch,
        compiler_params=pltpu.CompilerParams(
            collective_id=0, has_side_effects=True, vmem_limit_bytes=60 * 1024 * 1024
        ),
        cost_estimate=pl.CostEstimate(
            flops=1_300_000_000, bytes_accessed=22_000_000, transcendentals=0
        ),
    )(
        field_tiles,
        tile_dest.reshape(devices * BPD // 128, 128),
        near_cols.T,
        near_tiles,
        far_left.reshape(LEVELS * RANK, points),
        far_right.reshape(LEVELS * RANK, points),
    )


def solution(mesh):
    return jax.shard_map(
        shards,
        mesh=mesh,
        in_specs=(
            P(None, ("blk", "smp")),
            P(),
            P(("blk", "smp"), None),
            P(("blk", "smp"), None, None, None),
            P(None, None, ("blk", "smp")),
            P(None, None, ("blk", "smp")),
        ),
        out_specs=P(None, ("blk", "smp")),
        check_vma=False,
    )
```

```python
import functools

import jax
import jax.numpy as jnp
from jax import lax
from jax.experimental import pallas as pl
from jax.experimental.pallas import tpu as pltpu
from jax.sharding import PartitionSpec as P

BLOCK = 128
BPD = 64
RANK = 64
NEAR = 4
REACH = 8
LEVELS = 5
PARTS = 2
MESH = pl.DeviceIdType.MESH
F32 = jnp.float32
BF16 = jnp.bfloat16
NT = (((1,), (1,)), ((), ()))
NN = (((1,), (0,)), ((), ()))


def flipped(value, mask):
    bit = 1
    while bit <= mask:
        if mask & bit:
            value = value + bit - 2 * bit * ((value // bit) % 2)
        bit *= 2
    return value


def halves_swapped(x):
    return pltpu.roll(x, 64, 1)


def kernel(
    n_blk, n_smp, samples,
    field_h, dest_h, cols_h, near_h, left_h, right_h, out_ref,
    field_v, tiles_v, near_v, left_v, right_v, dest_v, cols_v, source_v, order_v, place_v,
    order_s, place_s, acc, proj,
    *rest,
):
    per = samples // PARTS
    half = per // 2
    peer = BPD // n_blk
    blk_bits = n_blk.bit_length() - 1
    smp_levels = LEVELS - blk_bits
    points = BPD * BLOCK
    rest = list(rest)

    def take(n):
        got = rest[:n]
        del rest[:n]
        return got

    outgoing, arrived, hil, low, high = (take(PARTS) for _ in range(5))
    z_send, z_recv, b_send, b_recv = (take(PARTS) for _ in range(4))
    load_sem, a2a_send, a2a_recv, halo_send, halo_recv = take(5)
    zs_sem, zr_sem, bs_sem, br_sem = take(4)

    blk = lax.axis_index("blk")
    smp = lax.axis_index("smp")
    me = blk * n_smp + smp

    def load(src, dst, at):
        copy = pltpu.make_async_copy(src, dst, load_sem.at[at])
        copy.start()
        return copy

    dest_load = load(dest_h, dest_v, 0)
    field_load = load(field_h, field_v, 1)
    cols_load = load(cols_h, cols_v, 2)

    following = ((blk + (smp + 1) // n_smp) % n_blk, (smp + 1) % n_smp)
    previous = (
        (blk + n_blk - 1 + (smp + n_smp - 1) // n_smp) % n_blk,
        (smp + n_smp - 1) % n_smp,
    )
    blk_peers = [(flipped(blk, j), smp) for j in range(1, n_blk)]
    smp_peers = [(blk, flipped(smp, j)) for j in range(1, n_smp)]
    everyone = blk_peers + smp_peers + [following, previous]
    barrier = pltpu.get_barrier_semaphore()
    for device in everyone:
        pl.semaphore_signal(barrier, inc=1, device_id=device, device_id_type=MESH)

    def load_parts(src, dst, at, parts):
        size = src.shape[0] // parts
        for i in range(parts):
            rows_i = pl.ds(i * size, size)
            load(src.at[rows_i], dst.at[rows_i], at)
        return pltpu.make_async_copy(src, dst, load_sem.at[at])

    right_load = load_parts(right_h, right_v, 3, 10)
    near_load = load_parts(near_h, near_v, 4, 16)
    left_load = load_parts(left_h, left_v, 5, 10)

    rows = lax.broadcasted_iota(jnp.int32, (BPD, 128), 0)
    lanes = lax.broadcasted_iota(jnp.int32, (BPD, 128), 1)
    dest_load.wait()
    own = jnp.broadcast_to(dest_v[pl.ds(me // 2, 1), :], (BPD, 128))
    own = jnp.where(lanes < BPD, pltpu.roll(own, 64 * (me % 2), 1), -1)
    target = lax.shift_right_arithmetic(own, (BPD * n_smp).bit_length() - 1)
    column = jnp.sum(jnp.where(rows == lanes, target, 0), axis=1, keepdims=True)
    before = jnp.where((target == column) & (lanes < rows), 1, 0)
    place = column * peer + jnp.sum(before, axis=1, keepdims=True)
    order = jnp.sum(jnp.where(place == lanes, rows, 0), axis=0, keepdims=True)
    order_v[...] = jnp.broadcast_to(order, (8, 128))
    order_copy = pltpu.make_async_copy(order_v, order_s, load_sem.at[6])
    order_copy.start()
    field_load.wait()

    def split(t, carry):
        at = pl.multiple_of(t * BLOCK, BLOCK)
        tiles_v[t] = field_v[:, pl.ds(at, BLOCK)]
        return carry

    lax.fori_loop(0, BPD, split, 0, unroll=8)
    order_copy.wait()

    def fill(part, j):
        group = flipped(blk, j)
        into = arrived[part] if j == 0 else outgoing[part]

        def body(i, carry):
            at = group * peer + i
            into[at] = tiles_v[order_s[0, at], pl.ds(part * per, per), :]
            return carry

        lax.fori_loop(0, peer, body, 0, unroll=True)

    def a2a(part, j):
        theirs = flipped(blk, j)
        return pltpu.make_async_remote_copy(
            src_ref=outgoing[part].at[pl.ds(theirs * peer, peer)],
            dst_ref=arrived[part].at[pl.ds(blk * peer, peer)],
            send_sem=a2a_send.at[part, j],
            recv_sem=a2a_recv.at[part, j],
            device_id=(theirs, smp),
            device_id_type=MESH,
        )

    sends = list(range(n_blk - 1, 0, -1))
    for at, j in enumerate(sends):
        fill(0, j)
        if at == 0:
            pl.semaphore_wait(barrier, len(everyone))
        a2a(0, j).start()
    for part in range(PARTS):
        fill(part, 0)
    for part in range(1, PARTS):
        for j in sends:
            fill(part, j)

    for s in range(n_blk):
        source_v[pl.ds(s, 1), :] = dest_v[pl.ds((s * n_smp + smp) // 2, 1), :]
    here = pltpu.roll(source_v[...], 64 * (smp % 2), 1) - me * BPD
    s_rows = lax.broadcasted_iota(jnp.int32, (n_blk, 128), 0)
    s_lanes = lax.broadcasted_iota(jnp.int32, (n_blk, 128), 1)
    here = jnp.where(s_lanes < BPD, here, -1)
    mine = jnp.where((here >= 0) & (here < BPD), 1, 0)
    total = mine
    shift = 1
    while shift < BPD:
        total = total + jnp.where(s_lanes >= shift, pltpu.roll(total, shift, 1), 0)
        shift *= 2
    lands = s_rows * peer + total - mine
    found = jnp.zeros((BPD, 128), jnp.int32)
    for s in range(n_blk):
        found = found + jnp.where(here[s : s + 1, :] == rows, lands[s : s + 1, :], 0)
    found = jnp.sum(found, axis=1, keepdims=True)
    found = jnp.sum(jnp.where(rows == lanes, found, 0), axis=0, keepdims=True)
    found = jnp.minimum(jnp.maximum(found, 0), BPD - 1)
    place_v[...] = jnp.broadcast_to(found, (8, 128))
    cols_load.wait()
    c_lanes = lax.broadcasted_iota(jnp.int32, (NEAR, BPD), 1)
    inner_row = (c_lanes >= REACH) & (c_lanes < BPD - REACH)
    base = jnp.where(inner_row, 0, jnp.where(c_lanes < REACH, -REACH, BPD - 2 * REACH))
    most = jnp.where(inner_row, BPD, 3 * REACH) - 1
    place_v[0:NEAR, 0:BPD] = jnp.minimum(jnp.maximum(cols_v[...] - me * BPD - base, 0), most)
    place_copy = pltpu.make_async_copy(place_v, place_s, load_sem.at[7])
    place_copy.start()
    place_copy.wait()

    lane = lax.broadcasted_iota(jnp.int32, (per, 128), 1) < 64
    lane_half = lax.broadcasted_iota(jnp.int32, (half, 128), 1) < 64

    def halo(part, up):
        source = hil[part].at[pl.ds(BPD - REACH, REACH) if up else pl.ds(0, REACH)]
        target_ref = low[part].at[pl.ds(0, REACH)] if up else high[part].at[pl.ds(2 * REACH, REACH)]
        return pltpu.make_async_remote_copy(
            src_ref=source,
            dst_ref=target_ref,
            send_sem=halo_send.at[part, int(up)],
            recv_sem=halo_recv.at[part, int(up)],
            device_id=following if up else previous,
            device_id_type=MESH,
        )

    def z_kind(j):
        return 1 if smp_levels and j == 1 else 0

    def z_copy(part, j):
        return pltpu.make_async_remote_copy(
            src_ref=z_send[part].at[z_kind(j)],
            dst_ref=z_recv[part].at[j],
            send_sem=zs_sem.at[part, j],
            recv_sem=zr_sem.at[part, j],
            device_id=(blk, flipped(smp, j)),
            device_id_type=MESH,
        )

    def b_level(j):
        return blk_bits - j.bit_length()

    def b_copy(part, j):
        return pltpu.make_async_remote_copy(
            src_ref=b_send[part].at[b_level(j)],
            dst_ref=b_recv[part].at[j],
            send_sem=bs_sem.at[part, j],
            recv_sem=br_sem.at[part, j],
            device_id=(flipped(blk, j), smp),
            device_id_type=MESH,
        )

    def gather(part):
        def edge(b, carry):
            first = arrived[part][place_s[NEAR, b]]
            hil[part][b] = first
            low[part][b + REACH] = first
            final = arrived[part][place_s[NEAR, b + BPD - 2 * REACH]]
            hil[part][b + BPD - 2 * REACH] = final
            high[part][b] = final
            return carry

        lax.fori_loop(0, 2 * REACH, edge, 0, unroll=4)
        halo(part, True).start()
        halo(part, False).start()

        def middle(b, carry):
            hil[part][b] = arrived[part][place_s[NEAR, b]]
            return carry

        lax.fori_loop(2 * REACH, BPD - 2 * REACH, middle, 0, unroll=4)

    def project(part):
        proj[...] = jnp.zeros_like(proj)
        group = 8

        def step(i, carry):
            b = i * group
            block = jnp.concatenate([hil[part][b + k] for k in range(group)], axis=1)
            at = pl.multiple_of(i * group * BLOCK, group * BLOCK)
            proj[0 : LEVELS * RANK, 0:per] += lax.dot_general(
                right_v[:, pl.ds(at, group * BLOCK)], block, NT, preferred_element_type=F32
            )
            return carry

        lax.fori_loop(0, BPD // group, step, 0)
        sums = proj[...].T[0:per, :]
        tiles = [sums[:, k * 128 : (k + 1) * 128] for k in range(3)]
        if smp_levels:
            other = jnp.where(lane, tiles[1], halves_swapped(tiles[2]))
            z_send[part][0] = jnp.concatenate(tiles[:2], axis=1).astype(BF16)
            z_send[part][1] = jnp.concatenate([tiles[0], other], axis=1).astype(BF16)
        else:
            z_send[part][0] = sums.astype(BF16)
        for j in range(n_smp - 1, 0, -1):
            z_copy(part, j).start()
        return tiles

    def packed(x, level):
        top, bottom = x[0:half], x[half:per]
        if level % 2 == 0:
            return jnp.where(lane_half, top, halves_swapped(bottom))
        return jnp.where(lane_half, halves_swapped(top), bottom)

    def unpacked(x, level):
        if level % 2 == 0:
            return jnp.concatenate([x, halves_swapped(x)], axis=0)
        return jnp.concatenate([halves_swapped(x), x], axis=0)

    def reduce_smp(part, tiles):
        for j in range(1, n_smp):
            z_copy(part, j).wait_recv()
        got = {j: z_recv[part][j].astype(F32) for j in range(1, n_smp)}
        for level in range(blk_bits):
            t = level // 2
            if level % 2 == 0:
                summed = tiles[t]
                for j in range(1, n_smp):
                    summed = summed + got[j][:, t * 128 : (t + 1) * 128]
            b_send[part][level] = packed(summed, level).astype(BF16)
        for j in sends:
            b_copy(part, j).start()
        if not smp_levels:
            return None
        return got[1][:, 128:256], got[2][:, 128:256] + got[3][:, 128:256]

    def couple(part, inner):
        for j in sends:
            b_copy(part, j).wait_recv()
        by_level = []
        for level in range(blk_bits):
            total = None
            for j in range(1, n_blk):
                if b_level(j) == level:
                    one = b_recv[part][j].astype(F32)
                    total = one if total is None else total + one
            by_level.append(unpacked(total, level))
        if smp_levels:
            by_level.append(inner[1])
            by_level.append(halves_swapped(inner[0]))
        devices = n_blk * n_smp
        scales = [(float(devices >> level + 1) * points) ** -0.5 for level in range(LEVELS)]
        by_level = [x * s for x, s in zip(by_level, scales)]
        first = jnp.where(lane, by_level[0], by_level[1]).astype(BF16)
        second = jnp.where(lane, by_level[2], by_level[3]).astype(BF16)
        third = by_level[4].astype(BF16)[:, 0:RANK]
        return jnp.concatenate([first, second], axis=1), third

    def near_rows(sources, start, stop):
        def body(b, carry):
            picks = []
            for k in range(NEAR):
                at = place_s[k, b]
                picks.append(jnp.concatenate([source[at] for source in sources], axis=0))
            picked = jnp.concatenate(picks, axis=1)
            tile = jnp.concatenate([near_v[b, k] for k in range(NEAR)], axis=1)
            acc[:, pl.ds(pl.multiple_of(b * BLOCK, BLOCK), BLOCK)] = lax.dot_general(
                picked, tile, NT, preferred_element_type=F32
            )
            return carry

        lax.fori_loop(start, stop, body, 0, unroll=4)

    wide = 512
    def far(couplings):
        first = jnp.concatenate([c[0] for c in couplings], axis=0)
        last = jnp.concatenate([c[1] for c in couplings], axis=0)

        def body(i, carry):
            at = pl.ds(pl.multiple_of(i * wide, wide), wide)
            value = lax.dot_general(
                first, left_v[0 : 4 * RANK, at], NN, preferred_element_type=F32
            ) + lax.dot_general(
                last, left_v[4 * RANK : 5 * RANK, at], NN, preferred_element_type=F32
            )
            out_ref[:, at] = (acc[:, at] + value).astype(BF16)
            return carry

        lax.fori_loop(0, points // wide, body, 0, unroll=4)

    tiles = [None] * PARTS
    inner = [None] * PARTS
    for part in range(PARTS):
        if part + 1 < PARTS:
            for j in sends:
                a2a(part, j).wait_send()
                a2a(part + 1, j).start()
        for j in sends:
            a2a(part, j).wait_recv()
        gather(part)
        if part == 0:
            right_load.wait()
        tiles[part] = project(part)
        if part > 0:
            inner[part - 1] = reduce_smp(part - 1, tiles[part - 1])
    near_load.wait()
    middle_row = BPD // 2
    near_rows(hil, REACH, middle_row)
    inner[PARTS - 1] = reduce_smp(PARTS - 1, tiles[PARTS - 1])
    near_rows(hil, middle_row, BPD - REACH)
    for part in range(PARTS):
        halo(part, True).wait_recv()
        halo(part, False).wait_recv()
    near_rows(low, 0, REACH)
    near_rows(high, BPD - REACH, BPD)
    left_load.wait()
    far([couple(part, inner[part]) for part in range(PARTS)])

    for j in sends:
        a2a(PARTS - 1, j).wait_send()
    for part in range(PARTS):
        halo(part, True).wait_send()
        halo(part, False).wait_send()
        for j in range(1, n_smp):
            z_copy(part, j).wait_send()
        for j in sends:
            b_copy(part, j).wait_send()


def shards(field_tiles, tile_dest, near_cols, near_tiles, far_left, far_right):
    samples, points = field_tiles.shape
    n_blk = lax.axis_size("blk")
    n_smp = lax.axis_size("smp")
    devices = n_blk * n_smp
    per = samples // PARTS
    blk_bits = n_blk.bit_length() - 1
    smp_levels = LEVELS - blk_bits
    z_wide = 256 if smp_levels else 384
    vmem = pltpu.VMEM
    dma = pltpu.SemaphoreType.DMA
    scratch = [
        vmem((samples, points), BF16),
        vmem((BPD, samples, BLOCK), BF16),
        vmem((BPD, NEAR, BLOCK, BLOCK), BF16),
        vmem((LEVELS * RANK, points), BF16),
        vmem((LEVELS * RANK, points), BF16),
        vmem((devices * BPD // 128, 128), jnp.int32),
        vmem((NEAR, BPD), jnp.int32),
        vmem((n_blk, 128), jnp.int32),
        vmem((8, 128), jnp.int32),
        vmem((8, 128), jnp.int32),
        pltpu.SMEM((8, 128), jnp.int32),
        pltpu.SMEM((8, 128), jnp.int32),
        vmem((samples, points), F32),
        vmem((384, 128), F32),
    ]
    scratch += [vmem((BPD, per, BLOCK), BF16) for _ in range(3 * PARTS)]
    scratch += [vmem((3 * REACH, per, BLOCK), BF16) for _ in range(2 * PARTS)]
    scratch += [vmem((2, per, z_wide), BF16) for _ in range(PARTS)]
    scratch += [vmem((n_smp, per, z_wide), BF16) for _ in range(PARTS)]
    scratch += [vmem((blk_bits, per // 2, 128), BF16) for _ in range(PARTS)]
    scratch += [vmem((n_blk, per // 2, 128), BF16) for _ in range(PARTS)]
    scratch += [
        dma((8,)),
        dma((PARTS, n_blk)), dma((PARTS, n_blk)),
        dma((PARTS, 2)), dma((PARTS, 2)),
        dma((PARTS, n_smp)), dma((PARTS, n_smp)),
        dma((PARTS, n_blk)), dma((PARTS, n_blk)),
    ]
    return pl.pallas_call(
        functools.partial(kernel, n_blk, n_smp, samples),
        out_shape=jax.ShapeDtypeStruct((samples, points), BF16),
        in_specs=[pl.BlockSpec(memory_space=pltpu.HBM)] * 6,
        out_specs=pl.BlockSpec(memory_space=vmem),
        scratch_shapes=scratch,
        compiler_params=pltpu.CompilerParams(
            collective_id=0, has_side_effects=True, vmem_limit_bytes=48 * 1024 * 1024
        ),
        cost_estimate=pl.CostEstimate(
            flops=1_300_000_000, bytes_accessed=22_000_000, transcendentals=0
        ),
    )(
        field_tiles,
        tile_dest.reshape(devices * BPD // 128, 128),
        near_cols.T,
        near_tiles,
        far_left.reshape(LEVELS * RANK, points),
        far_right.reshape(LEVELS * RANK, points),
    )


def solution(mesh):
    return jax.shard_map(
        shards,
        mesh=mesh,
        in_specs=(
            P(None, ("blk", "smp")),
            P(),
            P(("blk", "smp"), None),
            P(("blk", "smp"), None, None, None),
            P(None, None, ("blk", "smp")),
            P(None, None, ("blk", "smp")),
        ),
        out_specs=P(None, ("blk", "smp")),
        check_vma=False,
    )
```

```python
import functools

import jax
import jax.numpy as jnp
from jax import lax
from jax.experimental import pallas as pl
from jax.experimental.pallas import tpu as pltpu
from jax.sharding import PartitionSpec as P

BLOCK = 128
BPD = 64
RANK = 64
NEAR = 4
REACH = 8
LEVELS = 5
PARTS = 1
MESH = pl.DeviceIdType.MESH
F32 = jnp.float32
BF16 = jnp.bfloat16
NT = (((1,), (1,)), ((), ()))
NN = (((1,), (0,)), ((), ()))


def flipped(value, mask):
    bit = 1
    while bit <= mask:
        if mask & bit:
            value = value + bit - 2 * bit * ((value // bit) % 2)
        bit *= 2
    return value


def halves_swapped(x):
    return pltpu.roll(x, 64, 1)


def kernel(
    n_blk, n_smp, samples,
    field_h, dest_h, cols_h, near_h, left_h, right_h, out_h,
    field_v, tiles_v, near_v, left_v, right_v, dest_v, cols_v, source_v, order_v, place_v,
    order_s, place_s, acc, out_v, proj,
    *rest,
):
    per = samples // PARTS
    half = per // 2
    peer = BPD // n_blk
    blk_bits = n_blk.bit_length() - 1
    smp_levels = LEVELS - blk_bits
    points = BPD * BLOCK
    rest = list(rest)

    def take(n):
        got = rest[:n]
        del rest[:n]
        return got

    outgoing, arrived, hil, low, high = (take(PARTS) for _ in range(5))
    z_send, z_recv, b_send, b_recv = (take(PARTS) for _ in range(4))
    load_sem, a2a_send, a2a_recv, halo_send, halo_recv = take(5)
    zs_sem, zr_sem, bs_sem, br_sem, out_sem = take(5)

    blk = lax.axis_index("blk")
    smp = lax.axis_index("smp")
    me = blk * n_smp + smp

    def load(src, dst, at):
        copy = pltpu.make_async_copy(src, dst, load_sem.at[at])
        copy.start()
        return copy

    dest_load = load(dest_h, dest_v, 0)
    field_load = load(field_h, field_v, 1)
    cols_load = load(cols_h, cols_v, 2)

    following = ((blk + (smp + 1) // n_smp) % n_blk, (smp + 1) % n_smp)
    previous = (
        (blk + n_blk - 1 + (smp + n_smp - 1) // n_smp) % n_blk,
        (smp + n_smp - 1) % n_smp,
    )
    blk_peers = [(flipped(blk, j), smp) for j in range(1, n_blk)]
    smp_peers = [(blk, flipped(smp, j)) for j in range(1, n_smp)]
    everyone = blk_peers + smp_peers + [following, previous]
    barrier = pltpu.get_barrier_semaphore()
    for device in everyone:
        pl.semaphore_signal(barrier, inc=1, device_id=device, device_id_type=MESH)

    def right_block(b, carry):
        at = pl.multiple_of(b * BLOCK, BLOCK)
        load(right_h.at[:, pl.ds(at, BLOCK)], right_v.at[b], 3)
        return carry

    lax.fori_loop(0, BPD, right_block, 0)
    near_load = load(near_h, near_v, 4)
    left_load = load(left_h, left_v, 5)

    rows = lax.broadcasted_iota(jnp.int32, (BPD, 128), 0)
    lanes = lax.broadcasted_iota(jnp.int32, (BPD, 128), 1)
    dest_load.wait()
    own = jnp.broadcast_to(dest_v[pl.ds(me // 2, 1), :], (BPD, 128))
    own = jnp.where(lanes < BPD, pltpu.roll(own, 64 * (me % 2), 1), -1)
    target = lax.shift_right_arithmetic(own, (BPD * n_smp).bit_length() - 1)
    column = jnp.sum(jnp.where(rows == lanes, target, 0), axis=1, keepdims=True)
    before = jnp.where((target == column) & (lanes < rows), 1, 0)
    place = column * peer + jnp.sum(before, axis=1, keepdims=True)
    order = jnp.sum(jnp.where(place == lanes, rows, 0), axis=0, keepdims=True)
    order_v[...] = jnp.broadcast_to(order, (8, 128))
    order_copy = pltpu.make_async_copy(order_v, order_s, load_sem.at[6])
    order_copy.start()
    field_load.wait()

    def split(t, carry):
        at = pl.multiple_of(t * BLOCK, BLOCK)
        tiles_v[t] = field_v[:, pl.ds(at, BLOCK)]
        return carry

    lax.fori_loop(0, BPD, split, 0, unroll=8)
    order_copy.wait()

    def fill(part, j):
        group = flipped(blk, j)
        into = arrived[part] if j == 0 else outgoing[part]

        def body(i, carry):
            at = group * peer + i
            into[at] = tiles_v[order_s[0, at], pl.ds(part * per, per), :]
            return carry

        lax.fori_loop(0, peer, body, 0, unroll=True)

    def a2a(part, j):
        theirs = flipped(blk, j)
        return pltpu.make_async_remote_copy(
            src_ref=outgoing[part].at[pl.ds(theirs * peer, peer)],
            dst_ref=arrived[part].at[pl.ds(blk * peer, peer)],
            send_sem=a2a_send.at[part, j],
            recv_sem=a2a_recv.at[part, j],
            device_id=(theirs, smp),
            device_id_type=MESH,
        )

    sends = [j for j in (1, 2, 4, 6, 7, 3, 5) if j < n_blk]
    sends += [j for j in range(8, n_blk)]
    window = 4
    for at, j in enumerate(sends):
        fill(0, j)
        if at == 0:
            pl.semaphore_wait(barrier, len(everyone))
        if at < window:
            a2a(0, j).start()
    fill(0, 0)

    for s in range(n_blk):
        source_v[pl.ds(s, 1), :] = dest_v[pl.ds((s * n_smp + smp) // 2, 1), :]
    here = pltpu.roll(source_v[...], 64 * (smp % 2), 1) - me * BPD
    s_rows = lax.broadcasted_iota(jnp.int32, (n_blk, 128), 0)
    s_lanes = lax.broadcasted_iota(jnp.int32, (n_blk, 128), 1)
    here = jnp.where(s_lanes < BPD, here, -1)
    mine = jnp.where((here >= 0) & (here < BPD), 1, 0)
    total = mine
    shift = 1
    while shift < BPD:
        total = total + jnp.where(s_lanes >= shift, pltpu.roll(total, shift, 1), 0)
        shift *= 2
    lands = s_rows * peer + total - mine
    lands = jnp.where(mine > 0, lands, -1)
    found = jnp.zeros((BPD, 128), jnp.int32)
    block_of = jnp.zeros((BPD, 128), jnp.int32)
    for s in range(n_blk):
        here_s, lands_s = here[s : s + 1, :], lands[s : s + 1, :]
        found = found + jnp.where(here_s == rows, lands_s, 0)
        block_of = block_of + jnp.where(lands_s == rows, here_s, 0)

    def row_of(x):
        x = jnp.sum(x, axis=1, keepdims=True)
        x = jnp.sum(jnp.where(rows == lanes, x, 0), axis=0, keepdims=True)
        return jnp.minimum(jnp.maximum(x, 0), BPD - 1)

    place_v[...] = jnp.broadcast_to(row_of(found), (8, 128))
    place_v[NEAR + 1 : NEAR + 2, :] = row_of(block_of)
    cols_load.wait()
    c_lanes = lax.broadcasted_iota(jnp.int32, (NEAR, BPD), 1)
    inner_row = (c_lanes >= REACH) & (c_lanes < BPD - REACH)
    base = jnp.where(inner_row, 0, jnp.where(c_lanes < REACH, -REACH, BPD - 2 * REACH))
    most = jnp.where(inner_row, BPD, 3 * REACH) - 1
    place_v[0:NEAR, 0:BPD] = jnp.minimum(jnp.maximum(cols_v[...] - me * BPD - base, 0), most)
    place_copy = pltpu.make_async_copy(place_v, place_s, load_sem.at[7])
    place_copy.start()
    place_copy.wait()

    lane = lax.broadcasted_iota(jnp.int32, (per, 128), 1) < 64
    lane_half = lax.broadcasted_iota(jnp.int32, (half, 128), 1) < 64

    def halo(part, up):
        source = hil[part].at[pl.ds(BPD - REACH, REACH) if up else pl.ds(0, REACH)]
        target_ref = low[part].at[pl.ds(0, REACH)] if up else high[part].at[pl.ds(2 * REACH, REACH)]
        return pltpu.make_async_remote_copy(
            src_ref=source,
            dst_ref=target_ref,
            send_sem=halo_send.at[part, int(up)],
            recv_sem=halo_recv.at[part, int(up)],
            device_id=following if up else previous,
            device_id_type=MESH,
        )

    def z_kind(j):
        return 1 if smp_levels and j == 1 else 0

    def z_copy(part, j):
        return pltpu.make_async_remote_copy(
            src_ref=z_send[part].at[z_kind(j)],
            dst_ref=z_recv[part].at[j],
            send_sem=zs_sem.at[part, j],
            recv_sem=zr_sem.at[part, j],
            device_id=(blk, flipped(smp, j)),
            device_id_type=MESH,
        )

    def b_level(j):
        return blk_bits - j.bit_length()

    def b_copy(part, j):
        return pltpu.make_async_remote_copy(
            src_ref=b_send[part].at[b_level(j)],
            dst_ref=b_recv[part].at[j],
            send_sem=bs_sem.at[part, j],
            recv_sem=br_sem.at[part, j],
            device_id=(flipped(blk, j), smp),
            device_id_type=MESH,
        )

    def gather(part):
        def edge(b, carry):
            first = arrived[part][place_s[NEAR, b]]
            hil[part][b] = first
            low[part][b + REACH] = first
            final = arrived[part][place_s[NEAR, b + BPD - 2 * REACH]]
            hil[part][b + BPD - 2 * REACH] = final
            high[part][b] = final
            return carry

        lax.fori_loop(0, 2 * REACH, edge, 0, unroll=4)
        halo(part, True).start()
        halo(part, False).start()

        def middle(b, carry):
            hil[part][b] = arrived[part][place_s[NEAR, b]]
            return carry

        lax.fori_loop(2 * REACH, BPD - 2 * REACH, middle, 0, unroll=4)

    def project(part, j):
        first = flipped(blk, j) * peer
        wide_rows = [right_v[place_s[NEAR + 1, first + i]] for i in range(peer)]
        block = jnp.concatenate([arrived[part][first + i] for i in range(peer)], axis=1)
        proj[0 : LEVELS * RANK, 0:per] += lax.dot_general(
            jnp.concatenate(wide_rows, axis=1), block, NT, preferred_element_type=F32
        )

    def send_projections(part):
        sums = proj[...].T[0:per, :]
        tiles = [sums[:, k * 128 : (k + 1) * 128] for k in range(3)]
        if smp_levels:
            other = jnp.where(lane, tiles[1], halves_swapped(tiles[2]))
            z_send[part][0] = jnp.concatenate(tiles[:2], axis=1).astype(BF16)
            z_send[part][1] = jnp.concatenate([tiles[0], other], axis=1).astype(BF16)
        else:
            z_send[part][0] = sums.astype(BF16)
        for j in range(n_smp - 1, 0, -1):
            z_copy(part, j).start()
        return tiles

    def packed(x, level):
        top, bottom = x[0:half], x[half:per]
        if level % 2 == 0:
            return jnp.where(lane_half, top, halves_swapped(bottom))
        return jnp.where(lane_half, halves_swapped(top), bottom)

    def unpacked(x, level):
        if level % 2 == 0:
            return jnp.concatenate([x, halves_swapped(x)], axis=0)
        return jnp.concatenate([halves_swapped(x), x], axis=0)

    def reduce_smp(part, tiles):
        for j in range(1, n_smp):
            z_copy(part, j).wait_recv()
        got = {j: z_recv[part][j].astype(F32) for j in range(1, n_smp)}
        for level in range(blk_bits):
            t = level // 2
            if level % 2 == 0:
                summed = tiles[t]
                for j in range(1, n_smp):
                    summed = summed + got[j][:, t * 128 : (t + 1) * 128]
            b_send[part][level] = packed(summed, level)
        for j in sends:
            b_copy(part, j).start()
        if not smp_levels:
            return None
        return got[1][:, 128:256], got[2][:, 128:256] + got[3][:, 128:256]

    def couple(part, inner):
        for j in sends:
            b_copy(part, j).wait_recv()
        by_level = []
        for level in range(blk_bits):
            total = None
            for j in range(1, n_blk):
                if b_level(j) == level:
                    one = b_recv[part][j]
                    total = one if total is None else total + one
            by_level.append(unpacked(total, level))
        if smp_levels:
            by_level.append(inner[1])
            by_level.append(halves_swapped(inner[0]))
        devices = n_blk * n_smp
        scales = [(float(devices >> level + 1) * points) ** -0.5 for level in range(LEVELS)]
        by_level = [x * s for x, s in zip(by_level, scales)]
        first = jnp.where(lane, by_level[0], by_level[1]).astype(BF16)
        second = jnp.where(lane, by_level[2], by_level[3]).astype(BF16)
        third = by_level[4].astype(BF16)[:, 0:RANK]
        return jnp.concatenate([first, second], axis=1), third

    def near_rows(sources, start, stop):
        def body(b, carry):
            picks = []
            for k in range(NEAR):
                at = place_s[k, b]
                picks.append(jnp.concatenate([source[at] for source in sources], axis=0))
            picked = jnp.concatenate(picks, axis=1)
            tile = jnp.concatenate([near_v[b, k] for k in range(NEAR)], axis=1)
            acc[:, pl.ds(pl.multiple_of(b * BLOCK, BLOCK), BLOCK)] = lax.dot_general(
                picked, tile, NT, preferred_element_type=F32
            )
            return carry

        lax.fori_loop(start, stop, body, 0, unroll=4)

    wide = 512
    pieces = 4

    def out_copy(piece):
        where = (slice(None), pl.ds(piece * (points // pieces), points // pieces))
        return pltpu.make_async_copy(out_v.at[where], out_h.at[where], out_sem.at[piece])

    def far(couplings):
        first = jnp.concatenate([c[0] for c in couplings], axis=0)
        last = jnp.concatenate([c[1] for c in couplings], axis=0)

        def body(i, carry):
            at = pl.ds(pl.multiple_of(i * wide, wide), wide)
            value = lax.dot_general(
                first, left_v[0 : 4 * RANK, at], NN, preferred_element_type=F32
            ) + lax.dot_general(
                last, left_v[4 * RANK : 5 * RANK, at], NN, preferred_element_type=F32
            )
            out_v[:, at] = (acc[:, at] + value).astype(BF16)
            return carry

        for piece in range(pieces):
            steps = points // pieces // wide
            lax.fori_loop(piece * steps, (piece + 1) * steps, body, 0, unroll=2)
            out_copy(piece).start()

    tiles = [None] * PARTS
    inner = [None] * PARTS
    proj[...] = jnp.zeros_like(proj)
    pltpu.make_async_copy(right_v, right_v, load_sem.at[3]).wait()
    project(0, 0)
    for at, j in enumerate(sends):
        following_send = at + window - 1
        if at >= 1 and following_send < len(sends):
            a2a(0, sends[at]).wait_send()
            a2a(0, sends[following_send]).start()
        a2a(0, j).wait_recv()
        project(0, j)
    tiles[0] = send_projections(0)
    gather(0)
    near_load.wait()
    middle_row = BPD * 5 // 8
    near_rows(hil, REACH, middle_row)
    inner[PARTS - 1] = reduce_smp(PARTS - 1, tiles[PARTS - 1])
    near_rows(hil, middle_row, BPD - REACH)
    for part in range(PARTS):
        halo(part, True).wait_recv()
        halo(part, False).wait_recv()
    near_rows(low, 0, REACH)
    near_rows(high, BPD - REACH, BPD)
    left_load.wait()
    far([couple(part, inner[part]) for part in range(PARTS)])

    for at, j in enumerate(sends):
        if at < 1 or at + window - 1 >= len(sends):
            a2a(0, j).wait_send()
    for part in range(PARTS):
        halo(part, True).wait_send()
        halo(part, False).wait_send()
        for j in range(1, n_smp):
            z_copy(part, j).wait_send()
        for j in sends:
            b_copy(part, j).wait_send()
    for piece in range(pieces):
        out_copy(piece).wait()


def shards(field_tiles, tile_dest, near_cols, near_tiles, far_left, far_right):
    samples, points = field_tiles.shape
    n_blk = lax.axis_size("blk")
    n_smp = lax.axis_size("smp")
    devices = n_blk * n_smp
    per = samples // PARTS
    blk_bits = n_blk.bit_length() - 1
    smp_levels = LEVELS - blk_bits
    z_wide = 256 if smp_levels else 384
    vmem = pltpu.VMEM
    dma = pltpu.SemaphoreType.DMA
    scratch = [
        vmem((samples, points), BF16),
        vmem((BPD, samples, BLOCK), BF16),
        vmem((BPD, NEAR, BLOCK, BLOCK), BF16),
        vmem((LEVELS * RANK, points), BF16),
        vmem((BPD, LEVELS * RANK, BLOCK), BF16),
        vmem((devices * BPD // 128, 128), jnp.int32),
        vmem((NEAR, BPD), jnp.int32),
        vmem((n_blk, 128), jnp.int32),
        vmem((8, 128), jnp.int32),
        vmem((8, 128), jnp.int32),
        pltpu.SMEM((8, 128), jnp.int32),
        pltpu.SMEM((8, 128), jnp.int32),
        vmem((samples, points), F32),
        vmem((samples, points), BF16),
        vmem((384, 128), F32),
    ]
    scratch += [vmem((BPD, per, BLOCK), BF16) for _ in range(3 * PARTS)]
    scratch += [vmem((3 * REACH, per, BLOCK), BF16) for _ in range(2 * PARTS)]
    scratch += [vmem((2, per, z_wide), BF16) for _ in range(PARTS)]
    scratch += [vmem((n_smp, per, z_wide), BF16) for _ in range(PARTS)]
    scratch += [vmem((blk_bits, per // 2, 128), F32) for _ in range(PARTS)]
    scratch += [vmem((n_blk, per // 2, 128), F32) for _ in range(PARTS)]
    scratch += [
        dma((8,)),
        dma((PARTS, n_blk)), dma((PARTS, n_blk)),
        dma((PARTS, 2)), dma((PARTS, 2)),
        dma((PARTS, n_smp)), dma((PARTS, n_smp)),
        dma((PARTS, n_blk)), dma((PARTS, n_blk)),
        dma((4,)),
    ]
    anywhere = pl.BlockSpec(memory_space=pl.ANY)
    return pl.pallas_call(
        functools.partial(kernel, n_blk, n_smp, samples),
        out_shape=jax.ShapeDtypeStruct((samples, points), BF16),
        in_specs=[anywhere] * 6,
        out_specs=anywhere,
        scratch_shapes=scratch,
        compiler_params=pltpu.CompilerParams(
            collective_id=0, has_side_effects=True, vmem_limit_bytes=60 * 1024 * 1024
        ),
        cost_estimate=pl.CostEstimate(
            flops=1_300_000_000, bytes_accessed=22_000_000, transcendentals=0
        ),
    )(
        field_tiles,
        tile_dest.reshape(devices * BPD // 128, 128),
        near_cols.T,
        near_tiles,
        far_left.reshape(LEVELS * RANK, points),
        far_right.reshape(LEVELS * RANK, points),
    )


def solution(mesh):
    return jax.shard_map(
        shards,
        mesh=mesh,
        in_specs=(
            P(None, ("blk", "smp")),
            P(),
            P(("blk", "smp"), None),
            P(("blk", "smp"), None, None, None),
            P(None, None, ("blk", "smp")),
            P(None, None, ("blk", "smp")),
        ),
        out_specs=P(None, ("blk", "smp")),
        check_vma=False,
    )
```

```python
import functools

import jax
import jax.numpy as jnp
from jax import lax
from jax.experimental import pallas as pl
from jax.experimental.pallas import tpu as pltpu
from jax.sharding import PartitionSpec as P

BLOCK = 128
BPD = 64
RANK = 64
NEAR = 4
REACH = 8
LEVELS = 5
PARTS = 2
MESH = pl.DeviceIdType.MESH
F32 = jnp.float32
BF16 = jnp.bfloat16
NT = (((1,), (1,)), ((), ()))
NN = (((1,), (0,)), ((), ()))


def flipped(value, mask):
    bit = 1
    while bit <= mask:
        if mask & bit:
            value = value + bit - 2 * bit * ((value // bit) % 2)
        bit *= 2
    return value


def halves_swapped(x):
    return pltpu.roll(x, 64, 1)


def kernel(
    n_blk, n_smp, samples,
    field_h, dest_h, cols_h, near_h, left_h, right_h, out_h,
    field_v, tiles_v, near_v, left_v, right_v, dest_v, cols_v, source_v, order_v, place_v,
    order_s, place_s, acc, out_v, proj,
    *rest,
):
    per = samples // PARTS
    half = per // 2
    peer = BPD // n_blk
    blk_bits = n_blk.bit_length() - 1
    smp_levels = LEVELS - blk_bits
    points = BPD * BLOCK
    rest = list(rest)

    def take(n):
        got = rest[:n]
        del rest[:n]
        return got

    outgoing, arrived, hil, low, high = (take(PARTS) for _ in range(5))
    z_send, z_recv, b_send, b_recv = (take(PARTS) for _ in range(4))
    load_sem, a2a_send, a2a_recv, halo_send, halo_recv = take(5)
    zs_sem, zr_sem, bs_sem, br_sem, out_sem = take(5)

    blk = lax.axis_index("blk")
    smp = lax.axis_index("smp")
    me = blk * n_smp + smp

    def load(src, dst, at):
        copy = pltpu.make_async_copy(src, dst, load_sem.at[at])
        copy.start()
        return copy

    dest_load = load(dest_h, dest_v, 0)
    field_load = load(field_h, field_v, 1)
    cols_load = load(cols_h, cols_v, 2)

    following = ((blk + (smp + 1) // n_smp) % n_blk, (smp + 1) % n_smp)
    previous = (
        (blk + n_blk - 1 + (smp + n_smp - 1) // n_smp) % n_blk,
        (smp + n_smp - 1) % n_smp,
    )
    blk_peers = [(flipped(blk, j), smp) for j in range(1, n_blk)]
    smp_peers = [(blk, flipped(smp, j)) for j in range(1, n_smp)]
    everyone = blk_peers + smp_peers + [following, previous]
    barrier = pltpu.get_barrier_semaphore()
    for device in everyone:
        pl.semaphore_signal(barrier, inc=1, device_id=device, device_id_type=MESH)

    def right_block(b, carry):
        at = pl.multiple_of(b * BLOCK, BLOCK)
        load(right_h.at[:, pl.ds(at, BLOCK)], right_v.at[b], 3)
        return carry

    lax.fori_loop(0, BPD, right_block, 0)
    near_load = load(near_h, near_v, 4)
    left_load = load(left_h, left_v, 5)

    rows = lax.broadcasted_iota(jnp.int32, (BPD, 128), 0)
    lanes = lax.broadcasted_iota(jnp.int32, (BPD, 128), 1)
    dest_load.wait()
    own = jnp.broadcast_to(dest_v[pl.ds(me // 2, 1), :], (BPD, 128))
    own = jnp.where(lanes < BPD, pltpu.roll(own, 64 * (me % 2), 1), -1)
    target = lax.shift_right_arithmetic(own, (BPD * n_smp).bit_length() - 1)
    column = jnp.sum(jnp.where(rows == lanes, target, 0), axis=1, keepdims=True)
    before = jnp.where((target == column) & (lanes < rows), 1, 0)
    place = column * peer + jnp.sum(before, axis=1, keepdims=True)
    order = jnp.sum(jnp.where(place == lanes, rows, 0), axis=0, keepdims=True)
    order_v[...] = jnp.broadcast_to(order, (8, 128))
    order_copy = pltpu.make_async_copy(order_v, order_s, load_sem.at[6])
    order_copy.start()
    field_load.wait()

    def split(t, carry):
        at = pl.multiple_of(t * BLOCK, BLOCK)
        tiles_v[t] = field_v[:, pl.ds(at, BLOCK)]
        return carry

    lax.fori_loop(0, BPD, split, 0, unroll=8)
    order_copy.wait()

    def fill(part, j):
        group = flipped(blk, j)
        into = arrived[part] if j == 0 else outgoing[part]

        def body(i, carry):
            at = group * peer + i
            into[at] = tiles_v[order_s[0, at], pl.ds(part * per, per), :]
            return carry

        lax.fori_loop(0, peer, body, 0, unroll=True)

    def a2a(part, j):
        theirs = flipped(blk, j)
        return pltpu.make_async_remote_copy(
            src_ref=outgoing[part].at[pl.ds(theirs * peer, peer)],
            dst_ref=arrived[part].at[pl.ds(blk * peer, peer)],
            send_sem=a2a_send.at[part, j],
            recv_sem=a2a_recv.at[part, j],
            device_id=(theirs, smp),
            device_id_type=MESH,
        )

    sends = [j for j in (1, 2, 4, 6, 7, 3, 5) if j < n_blk]
    sends += [j for j in range(8, n_blk)]
    window = 5
    messages = [(part, j) for part in range(PARTS) for j in sends]
    for at, (part, j) in enumerate(messages):
        fill(part, j)
        if at == 0:
            pl.semaphore_wait(barrier, len(everyone))
        if at < window:
            a2a(part, j).start()
    for part in range(PARTS):
        fill(part, 0)

    for s in range(n_blk):
        source_v[pl.ds(s, 1), :] = dest_v[pl.ds((s * n_smp + smp) // 2, 1), :]
    here = pltpu.roll(source_v[...], 64 * (smp % 2), 1) - me * BPD
    s_rows = lax.broadcasted_iota(jnp.int32, (n_blk, 128), 0)
    s_lanes = lax.broadcasted_iota(jnp.int32, (n_blk, 128), 1)
    here = jnp.where(s_lanes < BPD, here, -1)
    mine = jnp.where((here >= 0) & (here < BPD), 1, 0)
    total = mine
    shift = 1
    while shift < BPD:
        total = total + jnp.where(s_lanes >= shift, pltpu.roll(total, shift, 1), 0)
        shift *= 2
    lands = s_rows * peer + total - mine
    lands = jnp.where(mine > 0, lands, -1)
    found = jnp.zeros((BPD, 128), jnp.int32)
    block_of = jnp.zeros((BPD, 128), jnp.int32)
    for s in range(n_blk):
        here_s, lands_s = here[s : s + 1, :], lands[s : s + 1, :]
        found = found + jnp.where(here_s == rows, lands_s, 0)
        block_of = block_of + jnp.where(lands_s == rows, here_s, 0)

    def row_of(x):
        x = jnp.sum(x, axis=1, keepdims=True)
        x = jnp.sum(jnp.where(rows == lanes, x, 0), axis=0, keepdims=True)
        return jnp.minimum(jnp.maximum(x, 0), BPD - 1)

    place_v[...] = jnp.broadcast_to(row_of(found), (8, 128))
    place_v[NEAR + 1 : NEAR + 2, :] = row_of(block_of)
    cols_load.wait()
    c_lanes = lax.broadcasted_iota(jnp.int32, (NEAR, BPD), 1)
    inner_row = (c_lanes >= REACH) & (c_lanes < BPD - REACH)
    base = jnp.where(inner_row, 0, jnp.where(c_lanes < REACH, -REACH, BPD - 2 * REACH))
    most = jnp.where(inner_row, BPD, 3 * REACH) - 1
    place_v[0:NEAR, 0:BPD] = jnp.minimum(jnp.maximum(cols_v[...] - me * BPD - base, 0), most)
    place_copy = pltpu.make_async_copy(place_v, place_s, load_sem.at[7])
    place_copy.start()
    place_copy.wait()

    lane = lax.broadcasted_iota(jnp.int32, (per, 128), 1) < 64
    lane_half = lax.broadcasted_iota(jnp.int32, (half, 128), 1) < 64

    def halo(part, up):
        source = hil[part].at[pl.ds(BPD - REACH, REACH) if up else pl.ds(0, REACH)]
        target_ref = low[part].at[pl.ds(0, REACH)] if up else high[part].at[pl.ds(2 * REACH, REACH)]
        return pltpu.make_async_remote_copy(
            src_ref=source,
            dst_ref=target_ref,
            send_sem=halo_send.at[part, int(up)],
            recv_sem=halo_recv.at[part, int(up)],
            device_id=following if up else previous,
            device_id_type=MESH,
        )

    def z_kind(j):
        return 1 if smp_levels and j == 1 else 0

    def z_copy(part, j):
        return pltpu.make_async_remote_copy(
            src_ref=z_send[part].at[z_kind(j)],
            dst_ref=z_recv[part].at[j],
            send_sem=zs_sem.at[part, j],
            recv_sem=zr_sem.at[part, j],
            device_id=(blk, flipped(smp, j)),
            device_id_type=MESH,
        )

    def b_level(j):
        return blk_bits - j.bit_length()

    def b_copy(part, j):
        return pltpu.make_async_remote_copy(
            src_ref=b_send[part].at[b_level(j)],
            dst_ref=b_recv[part].at[j],
            send_sem=bs_sem.at[part, j],
            recv_sem=br_sem.at[part, j],
            device_id=(flipped(blk, j), smp),
            device_id_type=MESH,
        )

    def gather(part):
        def edge(b, carry):
            first = arrived[part][place_s[NEAR, b]]
            hil[part][b] = first
            low[part][b + REACH] = first
            final = arrived[part][place_s[NEAR, b + BPD - 2 * REACH]]
            hil[part][b + BPD - 2 * REACH] = final
            high[part][b] = final
            return carry

        lax.fori_loop(0, 2 * REACH, edge, 0, unroll=4)
        halo(part, True).start()
        halo(part, False).start()

        def middle(b, carry):
            hil[part][b] = arrived[part][place_s[NEAR, b]]
            return carry

        lax.fori_loop(2 * REACH, BPD - 2 * REACH, middle, 0, unroll=4)

    def project(part, j):
        first = flipped(blk, j) * peer
        wide_rows = [right_v[place_s[NEAR + 1, first + i]] for i in range(peer)]
        block = jnp.concatenate([arrived[part][first + i] for i in range(peer)], axis=1)
        proj[0 : LEVELS * RANK, 0:per] += lax.dot_general(
            jnp.concatenate(wide_rows, axis=1), block, NT, preferred_element_type=F32
        )

    def send_projections(part):
        sums = proj[...].T[0:per, :]
        tiles = [sums[:, k * 128 : (k + 1) * 128] for k in range(3)]
        if smp_levels:
            other = jnp.where(lane, tiles[1], halves_swapped(tiles[2]))
            z_send[part][0] = jnp.concatenate(tiles[:2], axis=1).astype(BF16)
            z_send[part][1] = jnp.concatenate([tiles[0], other], axis=1).astype(BF16)
        else:
            z_send[part][0] = sums.astype(BF16)
        for j in range(n_smp - 1, 0, -1):
            z_copy(part, j).start()
        return tiles

    def packed(x, level):
        top, bottom = x[0:half], x[half:per]
        if level % 2 == 0:
            return jnp.where(lane_half, top, halves_swapped(bottom))
        return jnp.where(lane_half, halves_swapped(top), bottom)

    def unpacked(x, level):
        if level % 2 == 0:
            return jnp.concatenate([x, halves_swapped(x)], axis=0)
        return jnp.concatenate([halves_swapped(x), x], axis=0)

    def reduce_smp(part, tiles):
        for j in range(1, n_smp):
            z_copy(part, j).wait_recv()
        got = {j: z_recv[part][j].astype(F32) for j in range(1, n_smp)}
        for level in range(blk_bits):
            t = level // 2
            if level % 2 == 0:
                summed = tiles[t]
                for j in range(1, n_smp):
                    summed = summed + got[j][:, t * 128 : (t + 1) * 128]
            b_send[part][level] = packed(summed, level)
        for j in sends:
            b_copy(part, j).start()
        if not smp_levels:
            return None
        return got[1][:, 128:256], got[2][:, 128:256] + got[3][:, 128:256]

    def couple(part, inner):
        for j in sends:
            b_copy(part, j).wait_recv()
        by_level = []
        for level in range(blk_bits):
            total = None
            for j in range(1, n_blk):
                if b_level(j) == level:
                    one = b_recv[part][j]
                    total = one if total is None else total + one
            by_level.append(unpacked(total, level))
        if smp_levels:
            by_level.append(inner[1])
            by_level.append(halves_swapped(inner[0]))
        devices = n_blk * n_smp
        scales = [(float(devices >> level + 1) * points) ** -0.5 for level in range(LEVELS)]
        by_level = [x * s for x, s in zip(by_level, scales)]
        first = jnp.where(lane, by_level[0], by_level[1]).astype(BF16)
        second = jnp.where(lane, by_level[2], by_level[3]).astype(BF16)
        third = by_level[4].astype(BF16)[:, 0:RANK]
        return jnp.concatenate([first, second], axis=1), third

    def near_rows(sources, start, stop):
        def body(b, carry):
            picks = []
            for k in range(NEAR):
                at = place_s[k, b]
                picks.append(jnp.concatenate([source[at] for source in sources], axis=0))
            picked = jnp.concatenate(picks, axis=1)
            tile = jnp.concatenate([near_v[b, k] for k in range(NEAR)], axis=1)
            acc[:, pl.ds(pl.multiple_of(b * BLOCK, BLOCK), BLOCK)] = lax.dot_general(
                picked, tile, NT, preferred_element_type=F32
            )
            return carry

        lax.fori_loop(start, stop, body, 0, unroll=8)

    wide = 512
    pieces = 4

    def out_copy(piece):
        where = (slice(None), pl.ds(piece * (points // pieces), points // pieces))
        return pltpu.make_async_copy(out_v.at[where], out_h.at[where], out_sem.at[piece])

    def far(couplings):
        first = jnp.concatenate([c[0] for c in couplings], axis=0)
        last = jnp.concatenate([c[1] for c in couplings], axis=0)

        def body(i, carry):
            at = pl.ds(pl.multiple_of(i * wide, wide), wide)
            value = lax.dot_general(
                first, left_v[0 : 4 * RANK, at], NN, preferred_element_type=F32
            ) + lax.dot_general(
                last, left_v[4 * RANK : 5 * RANK, at], NN, preferred_element_type=F32
            )
            out_v[:, at] = (acc[:, at] + value).astype(BF16)
            return carry

        for piece in range(pieces):
            steps = points // pieces // wide
            lax.fori_loop(piece * steps, (piece + 1) * steps, body, 0, unroll=2)
            out_copy(piece).start()

    tiles = [None] * PARTS
    inner = [None] * PARTS
    proj[...] = jnp.zeros_like(proj)
    pltpu.make_async_copy(right_v, right_v, load_sem.at[3]).wait()
    project(0, 0)
    waited = set()
    for at, (part, j) in enumerate(messages):
        later = at + window - 1
        if at >= 1 and later < len(messages):
            waited.add(at)
            a2a(*messages[at]).wait_send()
            a2a(*messages[later]).start()
        a2a(part, j).wait_recv()
        project(part, j)
        if part > 0 and j == sends[3]:
            inner[part - 1] = reduce_smp(part - 1, tiles[part - 1])
        if j == sends[-1]:
            tiles[part] = send_projections(part)
            gather(part)
            if part + 1 < PARTS:
                proj[...] = jnp.zeros_like(proj)
                project(part + 1, 0)
    near_load.wait()
    middle_row = BPD * 5 // 8
    near_rows(hil, REACH, middle_row)
    inner[PARTS - 1] = reduce_smp(PARTS - 1, tiles[PARTS - 1])
    near_rows(hil, middle_row, BPD - REACH)
    for part in range(PARTS):
        halo(part, True).wait_recv()
        halo(part, False).wait_recv()
    near_rows(low, 0, REACH)
    near_rows(high, BPD - REACH, BPD)
    left_load.wait()
    far([couple(part, inner[part]) for part in range(PARTS)])

    for at, message in enumerate(messages):
        if at not in waited:
            a2a(*message).wait_send()
    for part in range(PARTS):
        halo(part, True).wait_send()
        halo(part, False).wait_send()
        for j in range(1, n_smp):
            z_copy(part, j).wait_send()
        for j in sends:
            b_copy(part, j).wait_send()
    for piece in range(pieces):
        out_copy(piece).wait()


def shards(field_tiles, tile_dest, near_cols, near_tiles, far_left, far_right):
    samples, points = field_tiles.shape
    n_blk = lax.axis_size("blk")
    n_smp = lax.axis_size("smp")
    devices = n_blk * n_smp
    per = samples // PARTS
    blk_bits = n_blk.bit_length() - 1
    smp_levels = LEVELS - blk_bits
    z_wide = 256 if smp_levels else 384
    vmem = pltpu.VMEM
    dma = pltpu.SemaphoreType.DMA
    scratch = [
        vmem((samples, points), BF16),
        vmem((BPD, samples, BLOCK), BF16),
        vmem((BPD, NEAR, BLOCK, BLOCK), BF16),
        vmem((LEVELS * RANK, points), BF16),
        vmem((BPD, LEVELS * RANK, BLOCK), BF16),
        vmem((devices * BPD // 128, 128), jnp.int32),
        vmem((NEAR, BPD), jnp.int32),
        vmem((n_blk, 128), jnp.int32),
        vmem((8, 128), jnp.int32),
        vmem((8, 128), jnp.int32),
        pltpu.SMEM((8, 128), jnp.int32),
        pltpu.SMEM((8, 128), jnp.int32),
        vmem((samples, points), F32),
        vmem((samples, points), BF16),
        vmem((384, 128), F32),
    ]
    scratch += [vmem((BPD, per, BLOCK), BF16) for _ in range(3 * PARTS)]
    scratch += [vmem((3 * REACH, per, BLOCK), BF16) for _ in range(2 * PARTS)]
    scratch += [vmem((2, per, z_wide), BF16) for _ in range(PARTS)]
    scratch += [vmem((n_smp, per, z_wide), BF16) for _ in range(PARTS)]
    scratch += [vmem((blk_bits, per // 2, 128), F32) for _ in range(PARTS)]
    scratch += [vmem((n_blk, per // 2, 128), F32) for _ in range(PARTS)]
    scratch += [
        dma((8,)),
        dma((PARTS, n_blk)), dma((PARTS, n_blk)),
        dma((PARTS, 2)), dma((PARTS, 2)),
        dma((PARTS, n_smp)), dma((PARTS, n_smp)),
        dma((PARTS, n_blk)), dma((PARTS, n_blk)),
        dma((4,)),
    ]
    anywhere = pl.BlockSpec(memory_space=pl.ANY)
    return pl.pallas_call(
        functools.partial(kernel, n_blk, n_smp, samples),
        out_shape=jax.ShapeDtypeStruct((samples, points), BF16),
        in_specs=[anywhere] * 6,
        out_specs=anywhere,
        scratch_shapes=scratch,
        compiler_params=pltpu.CompilerParams(
            collective_id=0, has_side_effects=True, vmem_limit_bytes=60 * 1024 * 1024
        ),
        cost_estimate=pl.CostEstimate(
            flops=1_300_000_000, bytes_accessed=22_000_000, transcendentals=0
        ),
    )(
        field_tiles,
        tile_dest.reshape(devices * BPD // 128, 128),
        near_cols.T,
        near_tiles,
        far_left.reshape(LEVELS * RANK, points),
        far_right.reshape(LEVELS * RANK, points),
    )


def solution(mesh):
    return jax.shard_map(
        shards,
        mesh=mesh,
        in_specs=(
            P(None, ("blk", "smp")),
            P(),
            P(("blk", "smp"), None),
            P(("blk", "smp"), None, None, None),
            P(None, None, ("blk", "smp")),
            P(None, None, ("blk", "smp")),
        ),
        out_specs=P(None, ("blk", "smp")),
        check_vma=False,
    )
```

```python
import functools

import jax
import jax.numpy as jnp
from jax import lax
from jax.experimental import pallas as pl
from jax.experimental.pallas import tpu as pltpu
from jax.sharding import PartitionSpec as P

BLOCK = 128
BPD = 64
RANK = 64
NEAR = 4
REACH = 8
LEVELS = 5
PARTS = 2
MESH = pl.DeviceIdType.MESH
F32 = jnp.float32
BF16 = jnp.bfloat16
NT = (((1,), (1,)), ((), ()))
NN = (((1,), (0,)), ((), ()))


def flipped(value, mask):
    bit = 1
    while bit <= mask:
        if mask & bit:
            value = value + bit - 2 * bit * ((value // bit) % 2)
        bit *= 2
    return value


def halves_swapped(x):
    return pltpu.roll(x, 64, 1)


def kernel(
    n_blk, n_smp, samples,
    field_h, dest_h, cols_h, near_h, left_h, right_h, out_ref,
    field_v, tiles_v, near_v, left_v, right_v, dest_v, cols_v, source_v, order_v, place_v,
    order_s, place_s, acc, proj,
    *rest,
):
    per = samples // PARTS
    half = per // 2
    peer = BPD // n_blk
    blk_bits = n_blk.bit_length() - 1
    smp_levels = LEVELS - blk_bits
    points = BPD * BLOCK
    rest = list(rest)

    def take(n):
        got = rest[:n]
        del rest[:n]
        return got

    outgoing, arrived, hil, low, high = (take(PARTS) for _ in range(5))
    z_send, z_recv, b_send, b_recv = (take(PARTS) for _ in range(4))
    load_sem, a2a_send, a2a_recv, halo_send, halo_recv = take(5)
    zs_sem, zr_sem, bs_sem, br_sem = take(4)

    blk = lax.axis_index("blk")
    smp = lax.axis_index("smp")
    me = blk * n_smp + smp

    def load(src, dst, at):
        copy = pltpu.make_async_copy(src, dst, load_sem.at[at])
        copy.start()
        return copy

    dest_load = load(dest_h, dest_v, 0)
    field_load = load(field_h, field_v, 1)
    cols_load = load(cols_h, cols_v, 2)

    following = ((blk + (smp + 1) // n_smp) % n_blk, (smp + 1) % n_smp)
    previous = (
        (blk + n_blk - 1 + (smp + n_smp - 1) // n_smp) % n_blk,
        (smp + n_smp - 1) % n_smp,
    )
    blk_peers = [(flipped(blk, j), smp) for j in range(1, n_blk)]
    smp_peers = [(blk, flipped(smp, j)) for j in range(1, n_smp)]
    everyone = blk_peers + smp_peers + [following, previous]
    barrier = pltpu.get_barrier_semaphore()
    for device in everyone:
        pl.semaphore_signal(barrier, inc=1, device_id=device, device_id_type=MESH)

    def right_block(b, carry):
        at = pl.multiple_of(b * BLOCK, BLOCK)
        load(right_h.at[:, pl.ds(at, BLOCK)], right_v.at[b], 3)
        return carry

    lax.fori_loop(0, BPD, right_block, 0)
    near_load = load(near_h, near_v, 4)
    left_load = load(left_h, left_v, 5)

    rows = lax.broadcasted_iota(jnp.int32, (BPD, 128), 0)
    lanes = lax.broadcasted_iota(jnp.int32, (BPD, 128), 1)
    dest_load.wait()
    own = jnp.broadcast_to(dest_v[pl.ds(me // 2, 1), :], (BPD, 128))
    own = jnp.where(lanes < BPD, pltpu.roll(own, 64 * (me % 2), 1), -1)
    target = lax.shift_right_arithmetic(own, (BPD * n_smp).bit_length() - 1)
    column = jnp.sum(jnp.where(rows == lanes, target, 0), axis=1, keepdims=True)
    before = jnp.where((target == column) & (lanes < rows), 1, 0)
    place = column * peer + jnp.sum(before, axis=1, keepdims=True)
    order = jnp.sum(jnp.where(place == lanes, rows, 0), axis=0, keepdims=True)
    order_v[...] = jnp.broadcast_to(order, (8, 128))
    order_copy = pltpu.make_async_copy(order_v, order_s, load_sem.at[6])
    order_copy.start()
    field_load.wait()

    def split(t, carry):
        at = pl.multiple_of(t * BLOCK, BLOCK)
        tiles_v[t] = field_v[:, pl.ds(at, BLOCK)]
        return carry

    lax.fori_loop(0, BPD, split, 0, unroll=8)
    order_copy.wait()

    def fill(part, j):
        group = flipped(blk, j)
        into = arrived[part] if j == 0 else outgoing[part]

        def body(i, carry):
            at = group * peer + i
            into[at] = tiles_v[order_s[0, at], pl.ds(part * per, per), :]
            return carry

        lax.fori_loop(0, peer, body, 0, unroll=True)

    def a2a(part, j):
        theirs = flipped(blk, j)
        return pltpu.make_async_remote_copy(
            src_ref=outgoing[part].at[pl.ds(theirs * peer, peer)],
            dst_ref=arrived[part].at[pl.ds(blk * peer, peer)],
            send_sem=a2a_send.at[part, j],
            recv_sem=a2a_recv.at[part, j],
            device_id=(theirs, smp),
            device_id_type=MESH,
        )

    sends = [j for j in (1, 2, 4, 6, 7, 3, 5) if j < n_blk]
    sends += [j for j in range(8, n_blk)]
    window = 5
    messages = [(part, j) for part in range(PARTS) for j in sends]
    for at, (part, j) in enumerate(messages):
        fill(part, j)
        if at == 0:
            pl.semaphore_wait(barrier, len(everyone))
        if at < window:
            a2a(part, j).start()
    for part in range(PARTS):
        fill(part, 0)

    for s in range(n_blk):
        source_v[pl.ds(s, 1), :] = dest_v[pl.ds((s * n_smp + smp) // 2, 1), :]
    here = pltpu.roll(source_v[...], 64 * (smp % 2), 1) - me * BPD
    s_rows = lax.broadcasted_iota(jnp.int32, (n_blk, 128), 0)
    s_lanes = lax.broadcasted_iota(jnp.int32, (n_blk, 128), 1)
    here = jnp.where(s_lanes < BPD, here, -1)
    mine = jnp.where((here >= 0) & (here < BPD), 1, 0)
    total = mine
    shift = 1
    while shift < BPD:
        total = total + jnp.where(s_lanes >= shift, pltpu.roll(total, shift, 1), 0)
        shift *= 2
    lands = s_rows * peer + total - mine
    lands = jnp.where(mine > 0, lands, -1)
    found = jnp.zeros((BPD, 128), jnp.int32)
    block_of = jnp.zeros((BPD, 128), jnp.int32)
    for s in range(n_blk):
        here_s, lands_s = here[s : s + 1, :], lands[s : s + 1, :]
        found = found + jnp.where(here_s == rows, lands_s, 0)
        block_of = block_of + jnp.where(lands_s == rows, here_s, 0)

    def row_of(x):
        x = jnp.sum(x, axis=1, keepdims=True)
        x = jnp.sum(jnp.where(rows == lanes, x, 0), axis=0, keepdims=True)
        return jnp.minimum(jnp.maximum(x, 0), BPD - 1)

    place_v[...] = jnp.broadcast_to(row_of(found), (8, 128))
    place_v[NEAR + 1 : NEAR + 2, :] = row_of(block_of)
    cols_load.wait()
    c_lanes = lax.broadcasted_iota(jnp.int32, (NEAR, BPD), 1)
    inner_row = (c_lanes >= REACH) & (c_lanes < BPD - REACH)
    base = jnp.where(inner_row, 0, jnp.where(c_lanes < REACH, -REACH, BPD - 2 * REACH))
    most = jnp.where(inner_row, BPD, 3 * REACH) - 1
    place_v[0:NEAR, 0:BPD] = jnp.minimum(jnp.maximum(cols_v[...] - me * BPD - base, 0), most)
    place_copy = pltpu.make_async_copy(place_v, place_s, load_sem.at[7])
    place_copy.start()
    place_copy.wait()

    lane = lax.broadcasted_iota(jnp.int32, (per, 128), 1) < 64
    lane_half = lax.broadcasted_iota(jnp.int32, (half, 128), 1) < 64

    def halo(part, up):
        source = hil[part].at[pl.ds(BPD - REACH, REACH) if up else pl.ds(0, REACH)]
        target_ref = low[part].at[pl.ds(0, REACH)] if up else high[part].at[pl.ds(2 * REACH, REACH)]
        return pltpu.make_async_remote_copy(
            src_ref=source,
            dst_ref=target_ref,
            send_sem=halo_send.at[part, int(up)],
            recv_sem=halo_recv.at[part, int(up)],
            device_id=following if up else previous,
            device_id_type=MESH,
        )

    def z_kind(j):
        return 1 if smp_levels and j == 1 else 0

    def z_copy(part, j):
        return pltpu.make_async_remote_copy(
            src_ref=z_send[part].at[z_kind(j)],
            dst_ref=z_recv[part].at[j],
            send_sem=zs_sem.at[part, j],
            recv_sem=zr_sem.at[part, j],
            device_id=(blk, flipped(smp, j)),
            device_id_type=MESH,
        )

    def b_level(j):
        return blk_bits - j.bit_length()

    def b_copy(part, j):
        return pltpu.make_async_remote_copy(
            src_ref=b_send[part].at[b_level(j)],
            dst_ref=b_recv[part].at[j],
            send_sem=bs_sem.at[part, j],
            recv_sem=br_sem.at[part, j],
            device_id=(flipped(blk, j), smp),
            device_id_type=MESH,
        )

    def gather(part):
        def edge(b, carry):
            first = arrived[part][place_s[NEAR, b]]
            hil[part][b] = first
            low[part][b + REACH] = first
            final = arrived[part][place_s[NEAR, b + BPD - 2 * REACH]]
            hil[part][b + BPD - 2 * REACH] = final
            high[part][b] = final
            return carry

        lax.fori_loop(0, 2 * REACH, edge, 0, unroll=4)
        halo(part, True).start()
        halo(part, False).start()

        def middle(b, carry):
            hil[part][b] = arrived[part][place_s[NEAR, b]]
            return carry

        lax.fori_loop(2 * REACH, BPD - 2 * REACH, middle, 0, unroll=4)

    def project(part, j):
        first = flipped(blk, j) * peer
        wide_rows = [right_v[place_s[NEAR + 1, first + i]] for i in range(peer)]
        block = jnp.concatenate([arrived[part][first + i] for i in range(peer)], axis=1)
        proj[0 : LEVELS * RANK, 0:per] += lax.dot_general(
            jnp.concatenate(wide_rows, axis=1), block, NT, preferred_element_type=F32
        )

    def send_projections(part):
        sums = proj[...].T[0:per, :]
        tiles = [sums[:, k * 128 : (k + 1) * 128] for k in range(3)]
        if smp_levels:
            other = jnp.where(lane, tiles[1], halves_swapped(tiles[2]))
            z_send[part][0] = jnp.concatenate(tiles[:2], axis=1).astype(BF16)
            z_send[part][1] = jnp.concatenate([tiles[0], other], axis=1).astype(BF16)
        else:
            z_send[part][0] = sums.astype(BF16)
        for j in range(n_smp - 1, 0, -1):
            z_copy(part, j).start()
        return tiles

    def packed(x, level):
        top, bottom = x[0:half], x[half:per]
        if level % 2 == 0:
            return jnp.where(lane_half, top, halves_swapped(bottom))
        return jnp.where(lane_half, halves_swapped(top), bottom)

    def unpacked(x, level):
        if level % 2 == 0:
            return jnp.concatenate([x, halves_swapped(x)], axis=0)
        return jnp.concatenate([halves_swapped(x), x], axis=0)

    def reduce_smp(part, tiles):
        for j in range(1, n_smp):
            z_copy(part, j).wait_recv()
        got = {j: z_recv[part][j].astype(F32) for j in range(1, n_smp)}
        for level in range(blk_bits):
            t = level // 2
            if level % 2 == 0:
                summed = tiles[t]
                for j in range(1, n_smp):
                    summed = summed + got[j][:, t * 128 : (t + 1) * 128]
            b_send[part][level] = packed(summed, level)
        for j in sends:
            b_copy(part, j).start()
        if not smp_levels:
            return None
        return got[1][:, 128:256], got[2][:, 128:256] + got[3][:, 128:256]

    def couple(part, inner):
        for j in sends:
            b_copy(part, j).wait_recv()
        by_level = []
        for level in range(blk_bits):
            total = None
            for j in range(1, n_blk):
                if b_level(j) == level:
                    one = b_recv[part][j]
                    total = one if total is None else total + one
            by_level.append(unpacked(total, level))
        if smp_levels:
            by_level.append(inner[1])
            by_level.append(halves_swapped(inner[0]))
        devices = n_blk * n_smp
        scales = [(float(devices >> level + 1) * points) ** -0.5 for level in range(LEVELS)]
        by_level = [x * s for x, s in zip(by_level, scales)]
        first = jnp.where(lane, by_level[0], by_level[1]).astype(BF16)
        second = jnp.where(lane, by_level[2], by_level[3]).astype(BF16)
        third = by_level[4].astype(BF16)[:, 0:RANK]
        return jnp.concatenate([first, second], axis=1), third

    def near_rows(sources, start, stop):
        def body(b, carry):
            picks = []
            for k in range(NEAR):
                at = place_s[k, b]
                picks.append(jnp.concatenate([source[at] for source in sources], axis=0))
            picked = jnp.concatenate(picks, axis=1)
            tile = jnp.concatenate([near_v[b, k] for k in range(NEAR)], axis=1)
            acc[:, pl.ds(pl.multiple_of(b * BLOCK, BLOCK), BLOCK)] = lax.dot_general(
                tile, picked, NT, preferred_element_type=F32
            ).T
            return carry

        lax.fori_loop(start, stop, body, 0, unroll=8)

    wide = 512
    def far(couplings):
        first = jnp.concatenate([c[0] for c in couplings], axis=0)
        last = jnp.concatenate([c[1] for c in couplings], axis=0)

        def body(i, carry):
            at = pl.ds(pl.multiple_of(i * wide, wide), wide)
            value = lax.dot_general(
                first, left_v[0 : 4 * RANK, at], NN, preferred_element_type=F32
            ) + lax.dot_general(
                last, left_v[4 * RANK : 5 * RANK, at], NN, preferred_element_type=F32
            )
            out_ref[:, at] = (acc[:, at] + value).astype(BF16)
            return carry

        lax.fori_loop(0, points // wide, body, 0, unroll=4)

    tiles = [None] * PARTS
    inner = [None] * PARTS
    proj[...] = jnp.zeros_like(proj)
    pltpu.make_async_copy(right_v, right_v, load_sem.at[3]).wait()
    project(0, 0)
    waited = set()
    for at, (part, j) in enumerate(messages):
        later = at + window - 1
        if at >= 1 and later < len(messages):
            waited.add(at)
            a2a(*messages[at]).wait_send()
            a2a(*messages[later]).start()
        a2a(part, j).wait_recv()
        project(part, j)
        if part > 0 and j == sends[3]:
            inner[part - 1] = reduce_smp(part - 1, tiles[part - 1])
        if j == sends[-1]:
            tiles[part] = send_projections(part)
            gather(part)
            if part + 1 < PARTS:
                proj[...] = jnp.zeros_like(proj)
                project(part + 1, 0)
    near_load.wait()
    middle_row = BPD * 5 // 8
    near_rows(hil, REACH, middle_row)
    inner[PARTS - 1] = reduce_smp(PARTS - 1, tiles[PARTS - 1])
    near_rows(hil, middle_row, BPD - REACH)
    for part in range(PARTS):
        halo(part, True).wait_recv()
        halo(part, False).wait_recv()
    near_rows(low, 0, REACH)
    near_rows(high, BPD - REACH, BPD)
    left_load.wait()
    far([couple(part, inner[part]) for part in range(PARTS)])

    for at, message in enumerate(messages):
        if at not in waited:
            a2a(*message).wait_send()
    for part in range(PARTS):
        halo(part, True).wait_send()
        halo(part, False).wait_send()
        for j in range(1, n_smp):
            z_copy(part, j).wait_send()
        for j in sends:
            b_copy(part, j).wait_send()


def shards(field_tiles, tile_dest, near_cols, near_tiles, far_left, far_right):
    samples, points = field_tiles.shape
    n_blk = lax.axis_size("blk")
    n_smp = lax.axis_size("smp")
    devices = n_blk * n_smp
    per = samples // PARTS
    blk_bits = n_blk.bit_length() - 1
    smp_levels = LEVELS - blk_bits
    z_wide = 256 if smp_levels else 384
    vmem = pltpu.VMEM
    dma = pltpu.SemaphoreType.DMA
    scratch = [
        vmem((samples, points), BF16),
        vmem((BPD, samples, BLOCK), BF16),
        vmem((BPD, NEAR, BLOCK, BLOCK), BF16),
        vmem((LEVELS * RANK, points), BF16),
        vmem((BPD, LEVELS * RANK, BLOCK), BF16),
        vmem((devices * BPD // 128, 128), jnp.int32),
        vmem((NEAR, BPD), jnp.int32),
        vmem((n_blk, 128), jnp.int32),
        vmem((8, 128), jnp.int32),
        vmem((8, 128), jnp.int32),
        pltpu.SMEM((8, 128), jnp.int32),
        pltpu.SMEM((8, 128), jnp.int32),
        vmem((samples, points), F32),
        vmem((384, 128), F32),
    ]
    scratch += [vmem((BPD, per, BLOCK), BF16) for _ in range(3 * PARTS)]
    scratch += [vmem((3 * REACH, per, BLOCK), BF16) for _ in range(2 * PARTS)]
    scratch += [vmem((2, per, z_wide), BF16) for _ in range(PARTS)]
    scratch += [vmem((n_smp, per, z_wide), BF16) for _ in range(PARTS)]
    scratch += [vmem((blk_bits, per // 2, 128), F32) for _ in range(PARTS)]
    scratch += [vmem((n_blk, per // 2, 128), F32) for _ in range(PARTS)]
    scratch += [
        dma((8,)),
        dma((PARTS, n_blk)), dma((PARTS, n_blk)),
        dma((PARTS, 2)), dma((PARTS, 2)),
        dma((PARTS, n_smp)), dma((PARTS, n_smp)),
        dma((PARTS, n_blk)), dma((PARTS, n_blk)),
    ]
    anywhere = pl.BlockSpec(memory_space=pl.ANY)
    return pl.pallas_call(
        functools.partial(kernel, n_blk, n_smp, samples),
        out_shape=jax.ShapeDtypeStruct((samples, points), BF16),
        in_specs=[anywhere] * 6,
        out_specs=pl.BlockSpec(memory_space=vmem),
        scratch_shapes=scratch,
        compiler_params=pltpu.CompilerParams(
            collective_id=0, has_side_effects=True, vmem_limit_bytes=52 * 1024 * 1024
        ),
        cost_estimate=pl.CostEstimate(
            flops=1_300_000_000, bytes_accessed=22_000_000, transcendentals=0
        ),
    )(
        field_tiles,
        tile_dest.reshape(devices * BPD // 128, 128),
        near_cols.T,
        near_tiles,
        far_left.reshape(LEVELS * RANK, points),
        far_right.reshape(LEVELS * RANK, points),
    )


def solution(mesh):
    return jax.shard_map(
        shards,
        mesh=mesh,
        in_specs=(
            P(None, ("blk", "smp")),
            P(),
            P(("blk", "smp"), None),
            P(("blk", "smp"), None, None, None),
            P(None, None, ("blk", "smp")),
            P(None, None, ("blk", "smp")),
        ),
        out_specs=P(None, ("blk", "smp")),
        check_vma=False,
    )
```

```python
import functools

import jax
import jax.numpy as jnp
from jax import lax
from jax.experimental import pallas as pl
from jax.experimental.pallas import tpu as pltpu
from jax.sharding import PartitionSpec as P

BLOCK = 128
BPD = 64
RANK = 64
NEAR = 4
REACH = 8
LEVELS = 5
PARTS = 2
MESH = pl.DeviceIdType.MESH
F32 = jnp.float32
BF16 = jnp.bfloat16
NT = (((1,), (1,)), ((), ()))
NN = (((1,), (0,)), ((), ()))


def flipped(value, mask):
    bit = 1
    while bit <= mask:
        if mask & bit:
            value = value + bit - 2 * bit * ((value // bit) % 2)
        bit *= 2
    return value


def halves_swapped(x):
    return pltpu.roll(x, 64, 1)


def kernel(
    n_blk, n_smp, samples,
    field_h, dest_h, cols_h, near_h, left_h, right_h, out_ref,
    field_v, tiles_v, near_v, left_v, right_v, dest_v, cols_v, source_v, order_v, place_v,
    order_s, place_s, acc, proj,
    *rest,
):
    per = samples // PARTS
    half = per // 2
    peer = BPD // n_blk
    blk_bits = n_blk.bit_length() - 1
    smp_levels = LEVELS - blk_bits
    points = BPD * BLOCK
    rest = list(rest)

    def take(n):
        got = rest[:n]
        del rest[:n]
        return got

    outgoing, arrived, hil, low, high = (take(PARTS) for _ in range(5))
    z_send, z_recv, b_send, b_recv = (take(PARTS) for _ in range(4))
    load_sem, a2a_send, a2a_recv, halo_send, halo_recv = take(5)
    zs_sem, zr_sem, bs_sem, br_sem = take(4)

    blk = lax.axis_index("blk")
    smp = lax.axis_index("smp")
    me = blk * n_smp + smp

    def load(src, dst, at):
        copy = pltpu.make_async_copy(src, dst, load_sem.at[at])
        copy.start()
        return copy

    dest_load = load(dest_h, dest_v, 0)
    field_load = load(field_h, field_v, 1)
    cols_load = load(cols_h, cols_v, 2)

    following = ((blk + (smp + 1) // n_smp) % n_blk, (smp + 1) % n_smp)
    previous = (
        (blk + n_blk - 1 + (smp + n_smp - 1) // n_smp) % n_blk,
        (smp + n_smp - 1) % n_smp,
    )
    blk_peers = [(flipped(blk, j), smp) for j in range(1, n_blk)]
    smp_peers = [(blk, flipped(smp, j)) for j in range(1, n_smp)]
    everyone = blk_peers + smp_peers + [following, previous]
    barrier = pltpu.get_barrier_semaphore()
    for device in everyone:
        pl.semaphore_signal(barrier, inc=1, device_id=device, device_id_type=MESH)

    def right_block(b, carry):
        at = pl.multiple_of(b * BLOCK, BLOCK)
        load(right_h.at[:, pl.ds(at, BLOCK)], right_v.at[b], 3)
        return carry

    lax.fori_loop(0, BPD, right_block, 0)
    near_load = load(near_h, near_v, 4)
    left_load = load(left_h, left_v, 5)

    rows = lax.broadcasted_iota(jnp.int32, (BPD, 128), 0)
    lanes = lax.broadcasted_iota(jnp.int32, (BPD, 128), 1)
    dest_load.wait()
    own = jnp.broadcast_to(dest_v[pl.ds(me // 2, 1), :], (BPD, 128))
    own = jnp.where(lanes < BPD, pltpu.roll(own, 64 * (me % 2), 1), -1)
    target = lax.shift_right_arithmetic(own, (BPD * n_smp).bit_length() - 1)
    column = jnp.sum(jnp.where(rows == lanes, target, 0), axis=1, keepdims=True)
    before = jnp.where((target == column) & (lanes < rows), 1, 0)
    place = column * peer + jnp.sum(before, axis=1, keepdims=True)
    order = jnp.sum(jnp.where(place == lanes, rows, 0), axis=0, keepdims=True)
    order_v[...] = jnp.broadcast_to(order, (8, 128))
    order_copy = pltpu.make_async_copy(order_v, order_s, load_sem.at[6])
    order_copy.start()
    field_load.wait()

    def split(t, carry):
        at = pl.multiple_of(t * BLOCK, BLOCK)
        tiles_v[t] = field_v[:, pl.ds(at, BLOCK)]
        return carry

    lax.fori_loop(0, BPD, split, 0, unroll=8)
    order_copy.wait()

    def fill(part, j):
        group = flipped(blk, j)
        into = arrived[part] if j == 0 else outgoing[part]

        def body(i, carry):
            at = group * peer + i
            into[at] = tiles_v[order_s[0, at], pl.ds(part * per, per), :]
            return carry

        lax.fori_loop(0, peer, body, 0, unroll=True)

    def a2a(part, j):
        theirs = flipped(blk, j)
        return pltpu.make_async_remote_copy(
            src_ref=outgoing[part].at[pl.ds(theirs * peer, peer)],
            dst_ref=arrived[part].at[pl.ds(blk * peer, peer)],
            send_sem=a2a_send.at[part, j],
            recv_sem=a2a_recv.at[part, j],
            device_id=(theirs, smp),
            device_id_type=MESH,
        )

    sends = [j for j in (1, 2, 4, 6, 7, 3, 5) if j < n_blk]
    sends += [j for j in range(8, n_blk)]
    window = 8
    messages = [(part, j) for part in range(PARTS) for j in sends]
    for at, (part, j) in enumerate(messages):
        fill(part, j)
        if at == 0:
            pl.semaphore_wait(barrier, len(everyone))
        if at < window:
            a2a(part, j).start()
    for part in range(PARTS):
        fill(part, 0)

    for s in range(n_blk):
        source_v[pl.ds(s, 1), :] = dest_v[pl.ds((s * n_smp + smp) // 2, 1), :]
    here = pltpu.roll(source_v[...], 64 * (smp % 2), 1) - me * BPD
    s_rows = lax.broadcasted_iota(jnp.int32, (n_blk, 128), 0)
    s_lanes = lax.broadcasted_iota(jnp.int32, (n_blk, 128), 1)
    here = jnp.where(s_lanes < BPD, here, -1)
    mine = jnp.where((here >= 0) & (here < BPD), 1, 0)
    total = mine
    shift = 1
    while shift < BPD:
        total = total + jnp.where(s_lanes >= shift, pltpu.roll(total, shift, 1), 0)
        shift *= 2
    lands = s_rows * peer + total - mine
    lands = jnp.where(mine > 0, lands, -1)
    found = jnp.zeros((BPD, 128), jnp.int32)
    block_of = jnp.zeros((BPD, 128), jnp.int32)
    for s in range(n_blk):
        here_s, lands_s = here[s : s + 1, :], lands[s : s + 1, :]
        found = found + jnp.where(here_s == rows, lands_s, 0)
        block_of = block_of + jnp.where(lands_s == rows, here_s, 0)

    def row_of(x):
        x = jnp.sum(x, axis=1, keepdims=True)
        x = jnp.sum(jnp.where(rows == lanes, x, 0), axis=0, keepdims=True)
        return jnp.minimum(jnp.maximum(x, 0), BPD - 1)

    place_v[...] = jnp.broadcast_to(row_of(found), (8, 128))
    place_v[NEAR + 1 : NEAR + 2, :] = row_of(block_of)
    cols_load.wait()
    c_lanes = lax.broadcasted_iota(jnp.int32, (NEAR, BPD), 1)
    inner_row = (c_lanes >= REACH) & (c_lanes < BPD - REACH)
    base = jnp.where(inner_row, 0, jnp.where(c_lanes < REACH, -REACH, BPD - 2 * REACH))
    most = jnp.where(inner_row, BPD, 3 * REACH) - 1
    place_v[0:NEAR, 0:BPD] = jnp.minimum(jnp.maximum(cols_v[...] - me * BPD - base, 0), most)
    place_copy = pltpu.make_async_copy(place_v, place_s, load_sem.at[7])
    place_copy.start()
    place_copy.wait()

    lane = lax.broadcasted_iota(jnp.int32, (per, 128), 1) < 64
    lane_half = lax.broadcasted_iota(jnp.int32, (half, 128), 1) < 64

    def halo(part, up):
        source = hil[part].at[pl.ds(BPD - REACH, REACH) if up else pl.ds(0, REACH)]
        target_ref = low[part].at[pl.ds(0, REACH)] if up else high[part].at[pl.ds(2 * REACH, REACH)]
        return pltpu.make_async_remote_copy(
            src_ref=source,
            dst_ref=target_ref,
            send_sem=halo_send.at[part, int(up)],
            recv_sem=halo_recv.at[part, int(up)],
            device_id=following if up else previous,
            device_id_type=MESH,
        )

    def z_kind(j):
        return 1 if smp_levels and j == 1 else 0

    def z_copy(part, j):
        return pltpu.make_async_remote_copy(
            src_ref=z_send[part].at[z_kind(j)],
            dst_ref=z_recv[part].at[j],
            send_sem=zs_sem.at[part, j],
            recv_sem=zr_sem.at[part, j],
            device_id=(blk, flipped(smp, j)),
            device_id_type=MESH,
        )

    def b_level(j):
        return blk_bits - j.bit_length()

    def b_copy(part, j):
        return pltpu.make_async_remote_copy(
            src_ref=b_send[part].at[b_level(j)],
            dst_ref=b_recv[part].at[j],
            send_sem=bs_sem.at[part, j],
            recv_sem=br_sem.at[part, j],
            device_id=(flipped(blk, j), smp),
            device_id_type=MESH,
        )

    def gather(part):
        def edge(b, carry):
            first = arrived[part][place_s[NEAR, b]]
            hil[part][b] = first
            low[part][b + REACH] = first
            final = arrived[part][place_s[NEAR, b + BPD - 2 * REACH]]
            hil[part][b + BPD - 2 * REACH] = final
            high[part][b] = final
            return carry

        lax.fori_loop(0, 2 * REACH, edge, 0, unroll=4)
        halo(part, True).start()
        halo(part, False).start()

        def middle(b, carry):
            hil[part][b] = arrived[part][place_s[NEAR, b]]
            return carry

        lax.fori_loop(2 * REACH, BPD - 2 * REACH, middle, 0, unroll=4)

    def project(part, j):
        first = flipped(blk, j) * peer
        wide_rows = [right_v[place_s[NEAR + 1, first + i]] for i in range(peer)]
        block = jnp.concatenate([arrived[part][first + i] for i in range(peer)], axis=1)
        proj[0 : LEVELS * RANK, 0:per] += lax.dot_general(
            jnp.concatenate(wide_rows, axis=1), block, NT, preferred_element_type=F32
        )

    def send_projections(part):
        sums = proj[...].T[0:per, :]
        tiles = [sums[:, k * 128 : (k + 1) * 128] for k in range(3)]
        if smp_levels:
            other = jnp.where(lane, tiles[1], halves_swapped(tiles[2]))
            z_send[part][0] = jnp.concatenate(tiles[:2], axis=1).astype(BF16)
            z_send[part][1] = jnp.concatenate([tiles[0], other], axis=1).astype(BF16)
        else:
            z_send[part][0] = sums.astype(BF16)
        for j in range(n_smp - 1, 0, -1):
            z_copy(part, j).start()
        return tiles

    def packed(x, level):
        top, bottom = x[0:half], x[half:per]
        if level % 2 == 0:
            return jnp.where(lane_half, top, halves_swapped(bottom))
        return jnp.where(lane_half, halves_swapped(top), bottom)

    def unpacked(x, level):
        if level % 2 == 0:
            return jnp.concatenate([x, halves_swapped(x)], axis=0)
        return jnp.concatenate([halves_swapped(x), x], axis=0)

    def reduce_smp(part, tiles):
        for j in range(1, n_smp):
            z_copy(part, j).wait_recv()
        got = {j: z_recv[part][j].astype(F32) for j in range(1, n_smp)}
        for level in range(blk_bits):
            t = level // 2
            if level % 2 == 0:
                summed = tiles[t]
                for j in range(1, n_smp):
                    summed = summed + got[j][:, t * 128 : (t + 1) * 128]
            b_send[part][level] = packed(summed, level)
        for j in sends:
            b_copy(part, j).start()
        if not smp_levels:
            return None
        return got[1][:, 128:256], got[2][:, 128:256] + got[3][:, 128:256]

    def couple(part, inner):
        for j in sends:
            b_copy(part, j).wait_recv()
        by_level = []
        for level in range(blk_bits):
            total = None
            for j in range(1, n_blk):
                if b_level(j) == level:
                    one = b_recv[part][j]
                    total = one if total is None else total + one
            by_level.append(unpacked(total, level))
        if smp_levels:
            by_level.append(inner[1])
            by_level.append(halves_swapped(inner[0]))
        devices = n_blk * n_smp
        scales = [(float(devices >> level + 1) * points) ** -0.5 for level in range(LEVELS)]
        by_level = [x * s for x, s in zip(by_level, scales)]
        first = jnp.where(lane, by_level[0], by_level[1]).astype(BF16)
        second = jnp.where(lane, by_level[2], by_level[3]).astype(BF16)
        third = by_level[4].astype(BF16)[:, 0:RANK]
        return jnp.concatenate([first, second], axis=1), third

    def near_rows(sources, start, stop):
        def body(b, carry):
            picks = []
            for k in range(NEAR):
                at = place_s[k, b]
                picks.append(jnp.concatenate([source[at] for source in sources], axis=0))
            picked = jnp.concatenate(picks, axis=1)
            tile = jnp.concatenate([near_v[b, k] for k in range(NEAR)], axis=1)
            acc[:, pl.ds(pl.multiple_of(b * BLOCK, BLOCK), BLOCK)] = lax.dot_general(
                tile, picked, NT, preferred_element_type=F32
            ).T
            return carry

        lax.fori_loop(start, stop, body, 0, unroll=8)

    wide = 512
    def far(couplings):
        first = jnp.concatenate([c[0] for c in couplings], axis=0)
        last = jnp.concatenate([c[1] for c in couplings], axis=0)

        def body(i, carry):
            at = pl.ds(pl.multiple_of(i * wide, wide), wide)
            value = lax.dot_general(
                first, left_v[0 : 4 * RANK, at], NN, preferred_element_type=F32
            ) + lax.dot_general(
                last, left_v[4 * RANK : 5 * RANK, at], NN, preferred_element_type=F32
            )
            out_ref[:, at] = (acc[:, at] + value).astype(BF16)
            return carry

        lax.fori_loop(0, points // wide, body, 0, unroll=4)

    tiles = [None] * PARTS
    inner = [None] * PARTS
    proj[...] = jnp.zeros_like(proj)
    pltpu.make_async_copy(right_v, right_v, load_sem.at[3]).wait()
    project(0, 0)
    waited = set()
    for at, (part, j) in enumerate(messages):
        later = at + window - 1
        if at >= 1 and later < len(messages):
            waited.add(at)
            a2a(*messages[at]).wait_send()
            a2a(*messages[later]).start()
        a2a(part, j).wait_recv()
        project(part, j)
        if part > 0 and j == sends[3]:
            inner[part - 1] = reduce_smp(part - 1, tiles[part - 1])
        if j == sends[-1]:
            tiles[part] = send_projections(part)
            gather(part)
            if part + 1 < PARTS:
                proj[...] = jnp.zeros_like(proj)
                project(part + 1, 0)
    near_load.wait()
    middle_row = BPD * 5 // 8
    near_rows(hil, REACH, middle_row)
    inner[PARTS - 1] = reduce_smp(PARTS - 1, tiles[PARTS - 1])
    near_rows(hil, middle_row, BPD - REACH)
    for part in range(PARTS):
        halo(part, True).wait_recv()
        halo(part, False).wait_recv()
    near_rows(low, 0, REACH)
    near_rows(high, BPD - REACH, BPD)
    left_load.wait()
    far([couple(part, inner[part]) for part in range(PARTS)])

    for at, message in enumerate(messages):
        if at not in waited:
            a2a(*message).wait_send()
    for part in range(PARTS):
        halo(part, True).wait_send()
        halo(part, False).wait_send()
        for j in range(1, n_smp):
            z_copy(part, j).wait_send()
        for j in sends:
            b_copy(part, j).wait_send()


def shards(field_tiles, tile_dest, near_cols, near_tiles, far_left, far_right):
    samples, points = field_tiles.shape
    n_blk = lax.axis_size("blk")
    n_smp = lax.axis_size("smp")
    devices = n_blk * n_smp
    per = samples // PARTS
    blk_bits = n_blk.bit_length() - 1
    smp_levels = LEVELS - blk_bits
    z_wide = 256 if smp_levels else 384
    vmem = pltpu.VMEM
    dma = pltpu.SemaphoreType.DMA
    scratch = [
        vmem((samples, points), BF16),
        vmem((BPD, samples, BLOCK), BF16),
        vmem((BPD, NEAR, BLOCK, BLOCK), BF16),
        vmem((LEVELS * RANK, points), BF16),
        vmem((BPD, LEVELS * RANK, BLOCK), BF16),
        vmem((devices * BPD // 128, 128), jnp.int32),
        vmem((NEAR, BPD), jnp.int32),
        vmem((n_blk, 128), jnp.int32),
        vmem((8, 128), jnp.int32),
        vmem((8, 128), jnp.int32),
        pltpu.SMEM((8, 128), jnp.int32),
        pltpu.SMEM((8, 128), jnp.int32),
        vmem((samples, points), F32),
        vmem((384, 128), F32),
    ]
    scratch += [vmem((BPD, per, BLOCK), BF16) for _ in range(3 * PARTS)]
    scratch += [vmem((3 * REACH, per, BLOCK), BF16) for _ in range(2 * PARTS)]
    scratch += [vmem((2, per, z_wide), BF16) for _ in range(PARTS)]
    scratch += [vmem((n_smp, per, z_wide), BF16) for _ in range(PARTS)]
    scratch += [vmem((blk_bits, per // 2, 128), F32) for _ in range(PARTS)]
    scratch += [vmem((n_blk, per // 2, 128), F32) for _ in range(PARTS)]
    scratch += [
        dma((8,)),
        dma((PARTS, n_blk)), dma((PARTS, n_blk)),
        dma((PARTS, 2)), dma((PARTS, 2)),
        dma((PARTS, n_smp)), dma((PARTS, n_smp)),
        dma((PARTS, n_blk)), dma((PARTS, n_blk)),
    ]
    anywhere = pl.BlockSpec(memory_space=pl.ANY)
    return pl.pallas_call(
        functools.partial(kernel, n_blk, n_smp, samples),
        out_shape=jax.ShapeDtypeStruct((samples, points), BF16),
        in_specs=[anywhere] * 6,
        out_specs=pl.BlockSpec(memory_space=vmem),
        scratch_shapes=scratch,
        compiler_params=pltpu.CompilerParams(
            collective_id=0, has_side_effects=True, vmem_limit_bytes=52 * 1024 * 1024
        ),
        cost_estimate=pl.CostEstimate(
            flops=1_300_000_000, bytes_accessed=22_000_000, transcendentals=0
        ),
    )(
        field_tiles,
        tile_dest.reshape(devices * BPD // 128, 128),
        near_cols.T,
        near_tiles,
        far_left.reshape(LEVELS * RANK, points),
        far_right.reshape(LEVELS * RANK, points),
    )


def solution(mesh):
    return jax.shard_map(
        shards,
        mesh=mesh,
        in_specs=(
            P(None, ("blk", "smp")),
            P(),
            P(("blk", "smp"), None),
            P(("blk", "smp"), None, None, None),
            P(None, None, ("blk", "smp")),
            P(None, None, ("blk", "smp")),
        ),
        out_specs=P(None, ("blk", "smp")),
        check_vma=False,
    )
```
